32 devices in a mesh: fsdp: 8 (over y, x, core), tensor: 4 (over z).
Axes of the slice: x: 2, y: 2, z: 4, core: 2. Of those that a mesh axis runs over, the one named last changes fastest.
Arguments:
- student_in: bfloat16 [24576, 768], P('fsdp'), may hold values from -6 to 6
- teacher_in: bfloat16 [24576, 768], P('fsdp'), may hold values from -6 to 6
- bucket_size: int32 [384], P('fsdp'), may hold values from 64 to 256, as said below
- seq_length: int32 [384], P('fsdp'), may hold values from 33 to 256, as said below
- qkv_latent: float32 [3, 768, 768], P(None, 'fsdp', 'tensor'), may hold values from -7.2 to 7.2
- out_latent: float32 [768, 768], P('tensor', 'fsdp'), may hold values from -7.2 to 7.2
- up_latent: float32 [768, 3072], P('fsdp', 'tensor'), may hold values from -7.2 to 7.2
- down_latent: float32 [3072, 768], P('tensor', 'fsdp'), may hold values from -7.2 to 7.2
- gain_attn: bfloat16 [768], P('fsdp'), may hold values from 0.25 to 1.75
- gain_ffn: bfloat16 [768], P('fsdp'), may hold values from 0.25 to 1.75
- teach_qkv: bfloat16 [3, 768, 768], P(None, 'fsdp', 'tensor'), may hold values from -0.21875 to 0.21875
- teach_out: bfloat16 [768, 768], P('tensor', 'fsdp'), may hold values from -0.625 to 0.625
- teach_up: bfloat16 [768, 3072], P('fsdp', 'tensor'), may hold values from -0.21875 to 0.21875
- teach_down: bfloat16 [3072, 768], P('tensor', 'fsdp'), may hold values from -0.109375 to 0.109375
Outputs:
- student_out: bfloat16 [24576, 768], P('fsdp', 'tensor')
- teacher_out: bfloat16 [24576, 768], P('fsdp', 'tensor')
- input_grad: float32 [24576, 768], P('fsdp', 'tensor')
- grad_qkv: float32 [3, 768, 768], P(None, 'fsdp', 'tensor')
- grad_out: float32 [768, 768], P('tensor', 'fsdp')
- grad_up: float32 [768, 3072], P('fsdp', 'tensor')
- grad_down: float32 [3072, 768], P('tensor', 'fsdp')
- grad_gain_attn: float32 [768], P('fsdp')
- grad_gain_ffn: float32 [768], P('fsdp')
The draws below stay inside these ranges and needn't reach their ends.
Inputs may be any that keep to these rules, and one draw needn't show every extreme that they name: `bucket_size`: for each unit of 64 slots, the size (64, 128 or 256) of the bucket that holds it; a bucket of size s covers s / 64 units and starts at a slot that is a multiple of s. `seq_length`: for each unit, the live tokens of the sequence in its bucket, equal over the units of a bucket; a bucket of size s holds more than s / 2 and at most s, at its start.
All inputs are finite; a program needn't handle non-finite values.
Results may differ from the reference program's by a relative error of at most 0.02.
The reference program's roundings to bfloat16 on the way count: a program that leaves them out, or rounds other values in their place, can miss the bound.
Values may be sent and summed in bfloat16 or wider, within the bound.
No kernel may reach another device: no remote copies, remote signals or barrier semaphores. Data moves between devices by JAX's collectives and lax.ppermute only.
A program may use at most 256 MiB of HBM per device.

```python
import math
import jax
import jax.numpy as jnp
from jax import lax

D = 768
HEADS = 12
HEAD_DIM = 64
FF = 3072
BLOCK = 512
TOKENS = 24576


LAYOUTS = ((256, 256, 256, 256), (128, 128, 128, 128), (128, 128, 64, 64), (64, 64, 128, 128), (64, 64, 64, 64))


def bucket_layout(key):
    groups = TOKENS // 256
    pick = jax.random.randint(jax.random.fold_in(key, 101), (groups,), 0, 5)
    pick = pick.at[0].set(0).at[1].set(4)
    table = jnp.array(LAYOUTS, dtype=jnp.int32)
    return table[pick].reshape(-1)


def rising(key, shape, axis_index, trend):
    first, second = jax.random.split(key, 2)
    base = jax.random.uniform(first, shape, jnp.float32, -1.0, 1.0)
    count = shape[axis_index]
    along = jnp.arange(count, dtype=jnp.float32) / count
    rough = jax.random.uniform(second, (count,), jnp.float32, math.log(0.4), math.log(1.2))
    factor = jnp.exp(rough + trend * along)
    view = [1] * len(shape)
    view[axis_index] = count
    return base * factor.reshape(view)


def draw_bucket_size(key, part):
    sizes = bucket_layout(key)
    return sizes


def draw_seq_length(key, part):
    sizes = bucket_layout(key)
    key = jax.random.fold_in(key, 7)
    units = sizes.shape[0]
    index = jnp.arange(units, dtype=jnp.int32)
    span = sizes // 64
    first = index // span * span
    raw = jax.random.randint(key, (units,), 0, 128)
    half = sizes // 2
    length = half + 1 + raw[first] % half
    length = length.at[0:4].set(256)
    length = length.at[4].set(33)
    return length


def draw_qkv_latent(key, part):
    key = jax.random.fold_in(key, 11)
    return rising(key, (3, D, D), 1, math.log(3.0))


def draw_out_latent(key, part):
    key = jax.random.fold_in(key, 13)
    return rising(key, (D, D), 1, math.log(3.0))


def draw_up_latent(key, part):
    key = jax.random.fold_in(key, 17)
    return rising(key, (D, FF), 0, math.log(3.0))


def draw_down_latent(key, part):
    key = jax.random.fold_in(key, 19)
    return rising(key, (FF, D), 1, math.log(3.0))


def block_levels(stream_key, shape, cuts, smallest, largest):
    def one(position, blocks):
        draws = jax.random.uniform(jax.random.fold_in(jax.random.fold_in(stream_key, 6), position), (blocks,), jnp.float32, smallest / len(cuts), largest / len(cuts))
        return jnp.repeat(jnp.exp(draws), shape[position] // blocks).reshape((-1,) + (1,) * (len(shape) - position - 1))

    gain = one(*cuts[0])
    for cut in cuts[1:]:
        gain = gain * one(*cut)
    return gain


def normal_values(rng, shape, spread, reach, shards=(), kind=jnp.bfloat16):
    level = block_levels(rng, shape, shards, -0.22, 0.18) if shards else 1.0
    drawn = jax.random.normal(rng, shape, jnp.float32) * spread * level
    return jnp.minimum(jnp.maximum(drawn, -reach), reach).astype(kind)


def setup_inputs(seed: int = 0) -> dict:
    seeds = jax.random.split(jax.random.key(seed), 15)
    return {
        "student_in": normal_values(seeds[0], (TOKENS, D), 1.0, 6.0, ((0, 8),)),
        "teacher_in": normal_values(seeds[1], (TOKENS, D), 1.0, 6.0, ((0, 8),)),
        "bucket_size": draw_bucket_size(jax.random.fold_in(seeds[14], 71), 0),
        "seq_length": draw_seq_length(jax.random.fold_in(seeds[14], 71), 0),
        "qkv_latent": draw_qkv_latent(jax.random.fold_in(seeds[14], 71), 0),
        "out_latent": draw_out_latent(jax.random.fold_in(seeds[14], 71), 0),
        "up_latent": draw_up_latent(jax.random.fold_in(seeds[14], 71), 0),
        "down_latent": draw_down_latent(jax.random.fold_in(seeds[14], 71), 0),
        "gain_attn": jnp.clip(1.0 + 0.15 * jax.random.normal(seeds[8], (D,), jnp.float32), 0.25, 1.75).astype(jnp.bfloat16),
        "gain_ffn": jnp.clip(1.0 + 0.15 * jax.random.normal(seeds[9], (D,), jnp.float32), 0.25, 1.75).astype(jnp.bfloat16),
        "teach_qkv": normal_values(seeds[10], (3, D, D), D ** -0.5, 0.21875, ((1, 8), (2, 4))),
        "teach_out": normal_values(seeds[11], (D, D), (D // 8) ** -0.5, 0.625, ((0, 4), (1, 8))),
        "teach_up": normal_values(seeds[12], (D, FF), D ** -0.5, 0.21875, ((0, 8), (1, 4))),
        "teach_down": normal_values(seeds[13], (FF, D), FF ** -0.5, 0.109375, ((0, 4), (1, 8))),
    }


CLIP_RANGE = 2.5
ATT_WEIGHT = 0.015625
EPSILON = 1e-06
NEG_FILL = -1000000000.0

@jax.custom_vjp
def low(v):
    return lax.optimization_barrier(v.astype(jnp.bfloat16)).astype(jnp.float32)

@jax.custom_vjp
def low_back(v):
    return v

def low_keep(v):
    return (low(v), None)

def low_pass(kept, grad):
    return (grad,)

def back_keep(v):
    return (v, None)

def back_low(kept, grad):
    return (low(grad),)
low.defvjp(low_keep, low_pass)
low_back.defvjp(back_keep, back_low)

def matmul(left, right):
    return jnp.dot(left, right, precision=lax.Precision.HIGHEST, preferred_element_type=jnp.float32)

def soft_clip(value):
    return CLIP_RANGE * jnp.tanh(value / CLIP_RANGE)

def layer_norm(value):
    centre = value - lax.optimization_barrier(jnp.mean(value, axis=-1, keepdims=True))
    return centre * lax.rsqrt(lax.optimization_barrier(jnp.mean(centre * centre, axis=-1, keepdims=True)) + EPSILON)

def gelu_exact(value):
    return jax.nn.gelu(value, approximate=False)

def sign_ste(latent_live, latent_fixed):
    return jnp.clip(latent_live, -1.0, 1.0) - jnp.clip(latent_fixed, -1.0, 1.0) + jnp.sign(latent_fixed)

def slot_tables(bucket_size, seq_length):
    slots = jnp.arange(bucket_size.shape[0] * 64, dtype=jnp.int32)
    sizes = jnp.repeat(bucket_size, 64)
    lengths = jnp.repeat(seq_length, 64)
    begin = slots // sizes * sizes
    return (begin, slots - begin < lengths)

def key_mask(begin, live):
    return (begin[:, None] == begin[None, :]) & live[None, :]

def softmax_rows(scores, keep):
    masked = jnp.where(keep[None], scores, NEG_FILL)
    top = lax.optimization_barrier(jnp.max(masked, axis=-1, keepdims=True))
    expo = jnp.exp(masked - top)
    return expo / lax.optimization_barrier(jnp.sum(expo, axis=-1, keepdims=True))

def heads_of(value):
    return value.reshape(BLOCK, HEADS, HEAD_DIM)

def teacher_block(weights, x, begin, live):
    w_qkv, w_out, w_up, w_down = weights
    scale = HEAD_DIM ** (-0.5)
    entry = low(x)
    query = low(matmul(entry, w_qkv[0]))
    keys = low(matmul(entry, w_qkv[1]))
    value = low(matmul(entry, w_qkv[2]))
    scores = jnp.einsum('qhd,khd->hqk', heads_of(query), heads_of(keys), precision=lax.Precision.HIGHEST) * scale
    probs = low(softmax_rows(scores, key_mask(begin, live)))
    attended = jnp.einsum('hqk,khd->qhd', probs, heads_of(value), precision=lax.Precision.HIGHEST)
    attended = low(attended.reshape(BLOCK, D))
    h_first = layer_norm(x + matmul(attended, w_out))
    hidden = low(gelu_exact(matmul(low(h_first), w_up)))
    return (layer_norm(h_first + matmul(hidden, w_down)), heads_of(query), heads_of(keys))

def student_block(weights, betas, x, begin, live, y_teach, q_teach, k_teach):
    w_qkv, w_out, w_up, w_down, g_attn, g_ffn = weights
    beta_qkv, beta_out, beta_up, beta_down = betas
    scale = HEAD_DIM ** (-0.5)
    entry = low(soft_clip(x))
    projected = [heads_of(low(beta_qkv * low_back(matmul(entry, w_qkv[j])))) for j in range(3)]
    keep = key_mask(begin, live)
    raw = jnp.einsum('qhd,khd->hqk', projected[0], projected[1], precision=lax.Precision.HIGHEST)
    scores = low_back(raw) * scale
    probs = low(softmax_rows(scores, keep))
    attended = jnp.einsum('hqk,khd->qhd', probs, projected[2], precision=lax.Precision.HIGHEST)
    attended = low(low_back(attended.reshape(BLOCK, D)))
    h_first = layer_norm(x + beta_out * low_back(matmul(attended, w_out))) * g_attn
    middle = low(soft_clip(h_first))
    hidden = low(gelu_exact(beta_up * low_back(matmul(middle, w_up))))
    result = layer_norm(h_first + beta_down * low_back(matmul(hidden, w_down))) * g_ffn
    teach = jnp.einsum('qhd,khd->hqk', q_teach, k_teach, precision=lax.Precision.HIGHEST) * scale
    both = keep[None] & live[None, :, None]
    gap = jnp.where(both, scores - teach, 0.0)
    miss = jnp.where(live[:, None], result - y_teach, 0.0)
    loss = 0.5 * jnp.sum(miss * miss) + 0.5 * ATT_WEIGHT * jnp.sum(gap * gap)
    return (result, loss)

def reference(student_in, teacher_in, bucket_size, seq_length, qkv_latent, out_latent, up_latent, down_latent, gain_attn, gain_ffn, teach_qkv, teach_out, teach_up, teach_down):
    begin, live = slot_tables(bucket_size, seq_length)
    count = student_in.shape[0] // BLOCK
    begins = begin.reshape(count, BLOCK)
    lives = live.reshape(count, BLOCK)
    x_student = student_in.astype(jnp.float32).reshape(count, BLOCK, D)
    x_teacher = teacher_in.astype(jnp.float32).reshape(count, BLOCK, D)
    teacher_weights = (teach_qkv.astype(jnp.float32), teach_out.astype(jnp.float32), teach_up.astype(jnp.float32), teach_down.astype(jnp.float32))
    betas = (2.0 * jnp.mean(jnp.abs(qkv_latent)) / math.sqrt(D), 2.0 * jnp.mean(jnp.abs(out_latent)) / math.sqrt(D), 2.0 * jnp.mean(jnp.abs(up_latent)) / math.sqrt(D), 2.0 * jnp.mean(jnp.abs(down_latent)) / math.sqrt(FF))

    def total_loss(x_all, lat_qkv, lat_out, lat_up, lat_down, g_attn, g_ffn):
        weights = (sign_ste(lat_qkv, qkv_latent), sign_ste(lat_out, out_latent), sign_ste(lat_up, up_latent), sign_ste(lat_down, down_latent), g_attn, g_ffn)

        def step(total, pieces):
            x_here, x_teach, begin_here, live_here = pieces
            y_teach, q_teach, k_teach = teacher_block(teacher_weights, x_teach, begin_here, live_here)
            result, loss = student_block(weights, betas, x_here, begin_here, live_here, y_teach, q_teach, k_teach)
            return (total + loss, (result, y_teach))
        total, outputs = lax.scan(jax.checkpoint(step), jnp.zeros((), jnp.float32), (x_all, x_teacher, begins, lives))
        return (total, outputs)
    total, back, outputs = jax.vjp(total_loss, x_student, qkv_latent, out_latent, up_latent, down_latent, gain_attn.astype(jnp.float32), gain_ffn.astype(jnp.float32), has_aux=True)
    results, y_teach = outputs
    grads = back(jnp.ones_like(total))
    rows = count * BLOCK
    return (results.reshape(rows, D).astype(jnp.bfloat16), y_teach.reshape(rows, D).astype(jnp.bfloat16), grads[0].reshape(rows, D), grads[1], grads[2], grads[3], grads[4], grads[5], grads[6])
```

```python
import functools
import math
import types

import jax
import jax.numpy as jnp
from jax import lax
from jax.experimental import pallas as pl
from jax.experimental.pallas import tpu as pltpu
from jax.sharding import PartitionSpec as P

HEAD_DIM = 64
PAIR = 2 * HEAD_DIM
TILE = 256
CLIP_RANGE = 2.5
ATT_WEIGHT = 0.015625
EPSILON = 1e-06
NEG_FILL = -1000000000.0
LOW = jnp.bfloat16
WIDE = jnp.float32
FSDP = "fsdp"
TENSOR = "tensor"
VMEM_BYTES = 60 * 1024 * 1024
WEIGH = 5


IN_PLACE = pl.BlockSpec(memory_space=pl.ANY)
SCALARS = pl.BlockSpec(memory_space=pltpu.SMEM)


class Task:
    def __init__(self, stages):
        self.stages = stages
        self.arrays = None

    def go_on(self):
        try:
            got = next(self.stages) if self.arrays is None else self.stages.send(self.arrays)
            self.arrays = list(got)
        except StopIteration:
            self.arrays = ()

    def finish(self):
        while self.arrays != ():
            self.go_on()


class Order:
    def __init__(self):
        self.after = []
        self.landing = []
        self.shards = []

    def land(self, *tasks, only=None):
        for task in tasks:
            for k in range(len(task.arrays)):
                if only is None or only == k:
                    self.landing.append((task, k))

    def wait(self, *arrays):
        self.after = self.after + list(arrays)

    def fence(self):
        def kernel(out):
            out[...] = jnp.zeros((8, 128), WIDE)

        self.call("fence", kernel, [], [((8, 128), WIDE, whole(8, 128))])

    def call(self, name, kernel, ins, outs, grid=(1,), scratch=(), flops=0, moved=0, onto=()):
        waits = [value for value in self.after if not any(value is array for array in onto)]
        passed = [task.arrays[k] for task, k in self.landing]
        count, given = len(ins), len(outs)
        skip = len(onto) + len(passed) + len(waits)

        def wrapped(*refs):
            kernel(*refs[:count], *refs[count + skip : count + skip + given], *refs[count + skip + given + len(passed) :])

        aliases = {count + k: k for k in range(len(onto))}
        aliases.update({count + len(onto) + k: given + k for k in range(len(passed))})
        results = pl.pallas_call(
            wrapped,
            grid=grid,
            in_specs=[spec for _, spec in ins] + [IN_PLACE] * skip,
            out_specs=[spec for _, _, spec in outs] + [IN_PLACE] * len(passed),
            out_shape=[jax.ShapeDtypeStruct(shape, dtype) for shape, dtype, _ in outs]
            + [jax.ShapeDtypeStruct(array.shape, array.dtype) for array in passed],
            scratch_shapes=list(scratch),
            input_output_aliases=aliases,
            compiler_params=pltpu.CompilerParams(vmem_limit_bytes=VMEM_BYTES),
            cost_estimate=pl.CostEstimate(flops=flops * WEIGH, bytes_accessed=moved * WEIGH, transcendentals=0),
            name=name,
        )(*[array for array, _ in ins], *onto, *passed, *waits)
        rest = list(results[given:])
        for task, k in self.landing:
            task.arrays[k] = rest.pop(0)
        self.landing = []
        self.after = [results[0]]
        return list(results[:given])


def whole(*shape):
    return pl.BlockSpec(shape, lambda *_: (0,) * len(shape))


def swap(value, axis, bit):
    size = lax.axis_size(axis)
    return lax.ppermute(value, axis, [(i, i ^ bit) for i in range(size)])


def swap_first(value):
    return lax.ppermute(value, FSDP, [(i, i ^ (4 if i % 2 else 2)) for i in range(8)])


def swap_second(value):
    return lax.ppermute(value, FSDP, [(i, i ^ (2 if i % 2 else 4)) for i in range(8)])


def bits_of(axis):
    size = lax.axis_size(axis)
    bits = [1 << k for k in range(size.bit_length() - 1)]
    return [bits[0]] + bits[:0:-1] if bits else []


def order_of(axis):
    order = [0]
    for bit in reversed(bits_of(axis)):
        order = order + [o ^ bit for o in order]
    return order


def two_links(rows):
    return lax.axis_size(FSDP) == 8 and rows % 32 == 0


CHIP_ORDERS = ([0, 2, 4, 6, 1, 5, 3, 7], [0, 4, 2, 6, 1, 3, 5, 7])


def feature_order(depth):
    if not two_links(depth):
        return jnp.array(order_of(FSDP), jnp.int32)
    odd = lax.axis_index(FSDP) & 1
    return jnp.where(odd > 0, jnp.array(CHIP_ORDERS[1], jnp.int32), jnp.array(CHIP_ORDERS[0], jnp.int32))


def reorder(blocks, back):
    plain = order_of(FSDP)
    results = []
    for chip in CHIP_ORDERS:
        if back:
            results.append([blocks[chip.index(m)] for m in plain])
        else:
            results.append([blocks[plain.index(m)] for m in chip])
    odd = lax.axis_index(FSDP) & 1
    return [jnp.where(odd > 0, two, one) for one, two in zip(*results)]


def join_columns(run, name, arrays, moves, columns):
    rows = arrays[0].shape[0]

    def kernel(*refs):
        for k, source, target, count in moves:
            refs[-1][:, target : target + count] = refs[k][:, source : source + count]

    return run.call(
        name,
        kernel,
        [(array, whole(*array.shape)) for array in arrays],
        [((rows, columns), LOW, whole(rows, columns))],
        moved=4 * rows * columns,
    )[0]


def side_by_side(run, name, left, right):
    n = left.shape[1]
    return join_columns(run, name, [left, right], [(0, 0, 0, n), (1, 0, n, n)], 2 * n)


def rows_side_by_side(run, name, value, rows):
    total, n = value.shape
    count = total // rows

    def kernel(ref, out):
        for k in range(count):
            out[:, k * n : (k + 1) * n] = ref[k * rows : (k + 1) * rows]

    return run.call(
        name, kernel, [(value, whole(total, n))], [((rows, count * n), LOW, whole(rows, count * n))], moved=4 * total * n
    )[0]


def gather_weight(run, name, shard, finish, store):
    value = shard()
    run.shards.append(value)
    if finish is None:
        (got,) = yield [lax.all_gather(value, TENSOR, axis=0, tiled=True)]
        mine = rows_side_by_side(run, name + "_rows", got, value.shape[0])
    else:
        (got,) = yield [swap(value, TENSOR, 2)]
        value = side_by_side(run, name + "_join", value, got)
        (got,) = yield [swap(value, TENSOR, 1)]
        mine = finish(name + "_rows", value, got)
    if two_links(mine.shape[0]):
        sibling = swap(mine, FSDP, 1)
        first, first_other = yield [swap_first(mine), swap_first(sibling)]
        second = swap(first_other, FSDP, 1)
        second_other, both = yield [swap(first, FSDP, 1), swap_first(second)]
        both_other = swap(both, FSDP, 1)
        store((mine, first, second, both, sibling, second_other, first_other, both_other))
    else:
        for bit in reversed(bits_of(FSDP)):
            mine = jnp.concatenate([mine, swap(mine, FSDP, bit)], axis=0)
        store((mine,))


def add_low(left, right):
    return (left.astype(WIDE) + right.astype(WIDE)).astype(LOW)


def scatter_weight(run, name, left, right, split, store, beside=None, swaps=False):
    rows, width = left.shape
    fsdp = lax.axis_size(FSDP)
    depth = width // fsdp
    columns = right.shape[1]
    middle, half = width // 2, columns // 2
    step = half
    steps = half // step
    side = pl.BlockSpec((rows, step), lambda j: (0, j))
    cost = dict(flops=2 * rows * middle * columns, moved=2 * (rows * columns + 2 * middle * columns))
    added = []
    out_step = step
    if beside is not None:
        added = [(value, whole(8, width)) for value in beside]
        lanes = step // 2
        out_step = 2 * (lanes + 64)
        half = steps * out_step
        columns = 2 * half

    def product(left_ref, right_ref, sums, start):
        value = kernel_tn(left_ref[...], right_ref[...])
        if not sums:
            return value
        turned = [
            jnp.broadcast_to(jnp.sum(ref[:, start : start + middle], axis=0, keepdims=True), (128, middle)).T for ref in sums
        ]
        lane = lax.broadcasted_iota(jnp.int32, (middle, 128), 1)
        more = jnp.where(lane == 0, turned[0], jnp.where(lane == 1, turned[1], 0.0))[:, :64]
        return jnp.concatenate([value[:, :lanes], more, value[:, lanes:], more], axis=1)

    def far_kernel(left_ref, right_ref, *refs):
        refs[-1][...] = product(left_ref, right_ref, refs[:-1], middle).astype(LOW)

    far = run.call(
        name + "_far",
        far_kernel,
        [(left, pl.BlockSpec((rows, middle), lambda j: (0, 1))), (right, side)] + added,
        [((middle, columns), LOW, pl.BlockSpec((middle, out_step), lambda j: (0, j)))],
        grid=(2 * steps,),
        **cost,
    )[0]
    (got,) = yield [swap(far, FSDP, 1)]
    near_ins = [
        (left, pl.BlockSpec((rows, middle), lambda j: (0, 0))),
        (right, side),
        (got, pl.BlockSpec((middle, out_step), lambda j: (0, j))),
    ] + added
    if two_links(depth):
        one = ((depth, columns), LOW, whole(depth, columns))
        at = [slice(k * depth, (k + 1) * depth) for k in range(4)]

        def near_kernel(left_ref, right_ref, got_ref, *refs):
            keep, send = refs[-2:]
            total = (product(left_ref, right_ref, refs[:-2], 0) + got_ref[...].astype(WIDE)).astype(LOW)
            keep[at[0]], keep[at[1]] = total[at[0]], total[at[2]]
            send[at[0]], send[at[1]] = total[at[1]], total[at[3]]

        def second(keep, got, own, onward):
            own[...] = add_low(keep[at[0]], got[at[0]])
            onward[...] = add_low(keep[at[1]], got[at[1]])

        def third(own, got, *outs):
            n = columns // len(outs)
            for k, out in enumerate(outs):
                lanes = slice(k * n, (k + 1) * n)
                out[...] = add_low(own[:, lanes], got[:, lanes])

        def third_rows(where, own, got, out):
            n = columns // 4
            for k in range(4):
                lanes = slice(k * n, (k + 1) * n)
                row = pl.multiple_of(where[k] * depth, depth)
                out[pl.ds(row, depth)] = add_low(own[:, lanes], got[:, lanes])

        pair = ((2 * depth, columns), LOW, pl.BlockSpec((2 * depth, out_step), lambda j: (0, j)))
        keep, send = run.call(name + "_near", near_kernel, near_ins, [pair] * 2, grid=(2 * steps,), **cost)
        (got,) = yield [swap_first(send)]
        full = whole(2 * depth, columns)
        own, onward = run.call(name + "_add2", second, [(keep, full), (got, full)], [one] * 2, moved=6 * depth * columns)
        (got,) = yield [swap_second(onward)]
        ins = [(own, one[2]), (got, one[2])]
        if split is None:
            shape = (4 * depth, columns // 4)
            m = jnp.arange(4, dtype=jnp.int32) ^ lax.axis_index(TENSOR)
            places = (m & 1) * 2 + (m >> 1) if swaps else jnp.arange(4, dtype=jnp.int32)
            ins = [(places, SCALARS)] + ins
            here = run.call(name + "_add3", third_rows, ins, [(shape, LOW, whole(*shape))], moved=6 * depth * columns)[0]
        else:
            shape = (depth, half)
            here = run.call(name + "_add3", third, ins, [(shape, LOW, whole(*shape))] * 2, moved=6 * depth * columns)
    else:

        def near_kernel(left_ref, right_ref, got_ref, *refs):
            value = product(left_ref, right_ref, refs[:-1], 0)
            refs[-1][...] = (value + got_ref[...].astype(WIDE)).astype(LOW)

        here = run.call(
            name + "_near",
            near_kernel,
            near_ins,
            [((middle, columns), LOW, pl.BlockSpec((middle, out_step), lambda j: (0, j)))],
            grid=(2 * steps,),
            **cost,
        )[0].reshape(fsdp // 2, depth, columns)
        count = fsdp // 2
        for bit in bits_of(FSDP)[1:]:
            count //= 2
            (got,) = yield [swap(here[count:], FSDP, bit)]
            here = add_low(here[:count], got)
        if split is None:
            here = here[0].reshape(depth, 4, -1).transpose(1, 0, 2).reshape(4 * depth, -1)
            swaps = False
        else:
            here = (here[0, :, :half], here[0, :, half:])
    if split is None and swaps:
        split = lambda blocks: tuple(blocks.reshape(2, 2, depth, -1))
        here = (here,)
    if split is None:
        (here,) = yield [lax.psum_scatter(here, TENSOR, scatter_dimension=0, tiled=True)]
        store(here.astype(WIDE))
        return
    keep, send = split(*here)
    for bit in bits_of(TENSOR):
        (got,) = yield [swap(send, TENSOR, bit)]
        total = add_low(keep, got)
        keep, send = total[: total.shape[0] // 2], total[total.shape[0] // 2 :]
    store(total[0].astype(WIDE))


def gather_small(gains, sums, store):
    depth = gains.shape[1]
    block = jnp.concatenate([sums, jnp.pad(gains, ((0, 6), (0, 128 - depth)))], axis=0)[None]
    for bit in reversed(bits_of(FSDP)):
        (got,) = yield [swap(block, FSDP, bit)]
        block = jnp.concatenate([block, got], axis=0)
    parts = [block[k, 8:10, :depth] for k in range(block.shape[0])]
    gains = jnp.concatenate(reorder(parts, False) if two_links(depth) else parts, axis=1)
    sums = block[:, :8]
    while sums.shape[0] > 1:
        sums = sums[: sums.shape[0] // 2] + sums[sums.shape[0] // 2 :]
    sums = sums[0]
    for bit in bits_of(TENSOR):
        (got,) = yield [swap(sums, TENSOR, bit)]
        sums = sums + got
    store(gains, sums[0])


def leave_columns(run, name, value, dtype, store):
    size = lax.axis_size(TENSOR)
    (got,) = yield [lax.all_to_all(value, TENSOR, 0, 0, tiled=True)]
    columns, rows = got.shape[0] // size, got.shape[1]

    def kernel(ref, out):
        out[...] = ref[...].astype(dtype)

    store(
        run.call(
            name,
            kernel,
            [(got, pl.BlockSpec((columns, rows), lambda i: (i, 0)))],
            [((columns, size * rows), dtype, pl.BlockSpec((columns, rows), lambda i: (0, i)))],
            grid=(size,),
            moved=8 * columns * rows,
        )[0].T
    )


def put_turned(value, natural, out, tile):
    out[:, tile * TILE : (tile + 1) * TILE] = kernel_nt(natural[...], value).astype(LOW)


def dot(left, right):
    return jnp.dot(left, right, preferred_element_type=WIDE)


def dot_tn(left, right):
    return lax.dot_general(left, right, (((0,), (0,)), ((), ())), preferred_element_type=WIDE)


def dot_nt(left, right):
    return lax.dot_general(left, right, (((1,), (1,)), ((), ())), preferred_element_type=WIDE)


def soft_clip(value):
    return CLIP_RANGE * jnp.tanh(value / CLIP_RANGE)


def clip_slope(value):
    bent = jnp.tanh(value / CLIP_RANGE)
    return 1.0 - bent * bent


def norm_parts(value):
    centre = value - jnp.mean(value, axis=-1, keepdims=True)
    scale = lax.rsqrt(jnp.mean(centre * centre, axis=-1, keepdims=True) + EPSILON)
    return centre * scale, scale


def norm_back(grad, normed, scale):
    return scale * (
        grad
        - jnp.mean(grad, axis=-1, keepdims=True)
        - normed * jnp.mean(grad * normed, axis=-1, keepdims=True)
    )


def gelu_cdf(value):
    return 0.5 + 0.5 * lax.erf(value * math.sqrt(0.5))


def gelu_density(value):
    return jnp.exp(-0.5 * value * value) * (1.0 / math.sqrt(2.0 * math.pi))


def kernel_nt(left, right):
    return lax.dot_general(left, right, (((1,), (1,)), ((), ())), preferred_element_type=WIDE)


def kernel_tn(left, right):
    return lax.dot_general(left, right, (((0,), (0,)), ((), ())), preferred_element_type=WIDE)


def kernel_nn(left, right):
    return jnp.dot(left, right, preferred_element_type=WIDE)


def times_weight(run, name, left, parts, tiles, work, extras, outs):
    rows, width = left.shape
    base, stride = tiles[0], tiles[1] - tiles[0]
    count = len(parts)

    def kernel(*refs):
        weight = refs[-1]
        row = 0
        for block in refs[1 : 1 + count]:
            weight[pl.ds(row, block.shape[0])] = block[...]
            row += block.shape[0]
        for r in range(0, rows, TILE):
            here = pl.ds(r, TILE)
            values = work(kernel_nn(refs[0][here], weight[...]), refs[1 + count : 1 + count + len(extras)], here)
            for ref, value in zip(refs[1 + count + len(extras) : -1], values):
                ref[here] = value

    columns = width * len(tiles)
    return run.call(
        name,
        kernel,
        [(left, whole(rows, width))]
        + [(part, pl.BlockSpec((part.shape[0], width), lambda j: (0, base + stride * j))) for part in parts]
        + extras,
        [((rows, columns), dtype, pl.BlockSpec((rows, width), lambda j: (0, j))) for dtype in outs],
        grid=(len(tiles),),
        scratch=[pltpu.VMEM((width, width), LOW)],
        flops=2 * rows * width * columns,
        moved=2 * (rows * width + width * columns + len(outs) * rows * columns),
    )


def times_turned(run, name, left, parts, tiles, work, extras, late, outs):
    rows, wide = left.shape
    width = sum(part.shape[0] for part in parts)
    step = wide // len(tiles)
    base, stride = tiles[0], tiles[1] - tiles[0] if len(tiles) > 1 else 1
    count, more = len(parts), len(extras)
    sources, held = [], []
    for item in late:
        pieces, column = item if isinstance(item, tuple) else ([item], 0)
        columns = pieces[0].shape[1] if column == 0 and not isinstance(item, tuple) else width
        row = 0
        for piece in pieces:
            sources.append((piece, len(held), row, column, columns))
            row += piece.shape[0]
        held.append(pltpu.VMEM((row, columns), pieces[0].dtype))
    first_late = 1 + count + more
    first_out = first_late + len(sources)
    first_held = first_out + len(outs) + 2

    def kernel(*refs):
        total, weight = refs[first_out + len(outs)], refs[first_out + len(outs) + 1]
        scratch, sems = refs[first_held:-1], refs[-1]
        j = pl.program_id(0)
        copies = []
        for k, (piece, to, row, column, columns) in enumerate(sources):
            copies.append(
                pltpu.make_async_copy(
                    refs[first_late + k].at[:, pl.ds(column, columns)],
                    scratch[to].at[pl.ds(row, piece.shape[0])],
                    sems.at[k],
                )
            )

        @pl.when(j == 0)
        def _():
            for copy in copies:
                copy.start()

        row = 0
        for block in refs[1 : 1 + count]:
            weight[pl.ds(row, block.shape[0])] = block[...]
            row += block.shape[0]
        product = kernel_nt(refs[0][...], weight[...])

        @pl.when(j == 0)
        def _():
            total[...] = product

        @pl.when(j > 0)
        def _():
            total[...] = total[...] + product

        @pl.when(j == len(tiles) - 1)
        def _():
            for copy in copies:
                copy.wait()
            for tile in range(rows // TILE):
                work(
                    total[pl.ds(tile * TILE, TILE)],
                    list(refs[1 + count : first_late]) + list(scratch),
                    refs[first_out : first_out + len(outs)],
                    tile,
                )

    return run.call(
        name,
        kernel,
        [(left, pl.BlockSpec((rows, step), lambda j: (0, j)))]
        + [(part, pl.BlockSpec((part.shape[0], step), lambda j: (0, base + stride * j))) for part in parts]
        + extras
        + [(piece, IN_PLACE) for piece, _, _, _, _ in sources],
        [(shape, dtype, whole(*shape)) for shape, dtype in outs],
        grid=(len(tiles),),
        scratch=[pltpu.VMEM((rows, width), WIDE), pltpu.VMEM((width, step), LOW)]
        + held
        + [pltpu.SemaphoreType.DMA((max(len(sources), 1),))],
        flops=2 * rows * width * wide,
        moved=2 * (rows * wide + width * wide),
    )


def rows_at(tile):
    return pl.ds(tile * TILE, TILE)


def tile_rows(columns):
    return pl.BlockSpec((TILE, columns), lambda i: (i, 0))


def add_column_sums(ref, value, tile):
    total = jnp.sum(value.reshape(value.shape[0] // 8, 8, value.shape[1]), axis=0)
    ref[...] = total if tile == 0 else ref[...] + total


def both_heads(value):
    first = lax.broadcasted_iota(jnp.int32, (1, PAIR), 1) < HEAD_DIM
    zero = jnp.zeros((), value.dtype)
    return jnp.concatenate([jnp.where(first, value, zero), jnp.where(first, zero, value)], axis=0)


def own_heads(value):
    return jnp.concatenate([value[:HEAD_DIM, :TILE], value[HEAD_DIM:, TILE:]], axis=0).T


def attend_forward(qid, kid, qs, ks, vs, qt, kt, vt, os, ot, probs_out, gap_out):
    keep = kid[:, 0:1] == qid[0:1, :]
    both = keep & (qid[1:2, :] > 0)
    bias = jnp.where(keep, 0.0, NEG_FILL)
    bias = jnp.concatenate([bias, bias], axis=1)
    seen = jnp.where(both, 1.0, 0.0)
    seen = jnp.concatenate([seen, seen], axis=1)

    def soft(score):
        masked = score + bias
        expo = jnp.exp(masked - jnp.max(masked, axis=0, keepdims=True))
        return (expo * (1.0 / jnp.sum(expo, axis=0, keepdims=True))).astype(LOW)

    for p in range(qs.shape[1] // PAIR):
        here = slice(p * PAIR, (p + 1) * PAIR)
        score_s = kernel_nt(ks[:, here], both_heads(qs[:, here]))
        score_t = kernel_nt(kt[:, here], both_heads(qt[:, here]))
        gap_out[0, p] = ((score_s - score_t) * seen).astype(LOW)
        probs = soft(score_s)
        probs_out[0, p] = probs
        os[:, here] = own_heads(kernel_tn(vs[:, here], probs)).astype(LOW)
        ot[:, here] = own_heads(kernel_tn(vt[:, here], soft(score_t))).astype(LOW)


def attend_backward(betas, proj, grad, probs, gap, out):
    width = grad.shape[1]
    up = jnp.asarray(1.0 / ATT_WEIGHT, LOW)
    b = betas[0] * ATT_WEIGHT
    scale = HEAD_DIM ** (-0.5)
    for p in range(width // PAIR):
        at_q = slice(p * PAIR, (p + 1) * PAIR)
        at_k = slice(width + p * PAIR, width + (p + 1) * PAIR)
        at_v = slice(2 * width + p * PAIR, 2 * width + (p + 1) * PAIR)
        grad_two = both_heads(grad[:, at_q] * up)
        prob_low = probs[0, p]
        prob = prob_low.astype(WIDE)
        weighted = prob * kernel_nt(proj[:, at_v], grad_two)
        inner = jnp.sum(weighted, axis=0, keepdims=True)
        d_score = (weighted - prob * inner + gap[0, p].astype(WIDE)).astype(LOW)
        out[:, at_v] = (b * kernel_nn(prob_low, grad_two)).astype(LOW)
        out[:, at_k] = (b * kernel_nn(d_score, both_heads(proj[:, at_q]))).astype(LOW)
        out[:, at_q] = own_heads((b * scale) * kernel_tn(proj[:, at_k], d_score)).astype(LOW)


def run_forward(run, step, steps, onto, qid, kid, proj_s, proj_t):
    rows, wide = proj_s.shape
    width = wide // 3
    pairs = width // PAIR
    tiles = rows // TILE

    def part(j):
        return pl.BlockSpec((TILE, width // steps), lambda b: (b, j * steps + step))

    square = pl.BlockSpec((1, pairs // steps, TILE, 2 * TILE), lambda b: (b, step, 0, 0))
    return run.call(
        "attend_forward",
        attend_forward,
        [(qid, pl.BlockSpec((8, TILE), lambda b: (0, b))), (kid, pl.BlockSpec((TILE, 128), lambda b: (b, 0)))]
        + [(value, part(j)) for value in (proj_s, proj_t) for j in range(3)],
        [((rows, width), LOW, part(0))] * 2 + [((tiles, pairs, TILE, 2 * TILE), LOW, square)] * 2,
        grid=(tiles,),
        flops=32 * rows * TILE * width // steps,
        moved=8 * rows * wide // steps,
        onto=onto,
    )


def run_backward(run, betas, proj_s, grad, probs, gap):
    rows, wide = proj_s.shape
    width = wide // 3
    pairs = width // PAIR
    square = pl.BlockSpec((1, pairs, TILE, 2 * TILE), lambda b: (b, 0, 0, 0))
    return run.call(
        "attend_backward",
        attend_backward,
        [(betas, SCALARS), (proj_s, tile_rows(wide)), (grad, tile_rows(width)), (probs, square), (gap, square)],
        [((rows, wide), LOW, tile_rows(wide))],
        grid=(rows // TILE,),
        flops=16 * rows * TILE * width,
        moved=8 * rows * wide,
    )[0]


def body(
    student_in,
    teacher_in,
    bucket_size,
    seq_length,
    qkv_latent,
    out_latent,
    up_latent,
    down_latent,
    gain_attn,
    gain_ffn,
    teach_qkv,
    teach_out,
    teach_up,
    teach_down,
):
    width = student_in.shape[1]
    fsdp = lax.axis_size(FSDP)
    tensor = lax.axis_size(TENSOR)
    rows = student_in.shape[0] // tensor
    depth = width // fsdp
    hidden_width = up_latent.shape[1] * tensor
    my_fsdp = lax.axis_index(FSDP)
    my_tensor = lax.axis_index(TENSOR)
    first_row = my_tensor * rows
    order = feature_order(depth)
    order_t = order_of(TENSOR)

    have = types.SimpleNamespace()
    run = Order()

    def keep(name):
        def store(value):
            setattr(have, name, value)

        return store

    def go_on(*tasks):
        for task in tasks:
            task.go_on()

    def finish(*tasks):
        for task in tasks:
            task.finish()

    gains = jnp.stack([gain_attn, gain_ffn]).astype(WIDE)

    def magnitudes():
        latents = (qkv_latent.reshape(-1, qkv_latent.shape[2]), out_latent, up_latent, down_latent)

        def kernel(*refs):
            lane = lax.broadcasted_iota(jnp.int32, (8, 128), 1)
            total = jnp.zeros((8, 128), WIDE)
            for k in range(4):
                total = jnp.where(lane == k, jnp.sum(jnp.abs(refs[k][...])), total)
            refs[4][...] = total

        return run.call(
            "magnitudes", kernel, [(value, whole(*value.shape)) for value in latents], [((8, 128), WIDE, whole(8, 128))]
        )[0]

    def pack_qkv(value):
        return value.astype(LOW).transpose(1, 0, 2).reshape(depth, -1)

    part = width // tensor

    def finish_qkv(name, near, far):
        moves = []
        for p in range(tensor):
            for k in range(4):
                moves.append((p // 2, (p % 2) * 4 * part + k * part, k * width + p * part, part))
        return join_columns(run, name, [near, far], moves, 4 * width)

    narrow_tiles = [0, 1, 2]

    def wide_tiles(which):
        return [2 * p + which for p in range(tensor)]

    def signs(value):
        return jnp.sign(value).astype(LOW)


    def shard_tqkv():
        return jnp.concatenate([pack_qkv(teach_qkv), teach_out.T], axis=1)

    def shard_qkv():
        return jnp.concatenate([pack_qkv(signs(qkv_latent)), signs(out_latent).T], axis=1)

    def pack_signs(name, teach, latent):
        def kernel(teach_ref, latent_ref, out):
            value = latent_ref[...]
            n = value.shape[1]
            out[:, :n] = teach_ref[...]
            out[:, n:] = jnp.where(value > 0, 1.0, jnp.where(value < 0, -1.0, 0.0)).astype(LOW)

        r, n = teach.shape
        return run.call(
            name, kernel, [(teach, whole(r, n)), (latent, whole(r, n))], [((r, 2 * n), LOW, whole(r, 2 * n))]
        )[0]

    def shard_up():
        return pack_signs("pack_up", teach_up, up_latent)

    def shard_down():
        return pack_signs("pack_down", teach_down.T, down_latent.T)

    def small_store(all_gains, totals):
        have.first_gain = all_gains[0:1]
        have.second_gain = all_gains[1:2]
        factors = (
            2.0 / (3 * width * width) / math.sqrt(width),
            2.0 / (width * width) / math.sqrt(width),
            2.0 / (width * hidden_width) / math.sqrt(width),
            2.0 / (width * hidden_width) / math.sqrt(hidden_width),
        )
        have.betas = totals[:4] * jnp.array(factors, WIDE)

    packed = ((width, rows), LOW)

    def prepare():
        scalars = jnp.concatenate([my_tensor.reshape(1), order ^ my_fsdp]).astype(jnp.int32)

        def kernel(where, student, teacher, x_low, entry, xt_low, to_place, rows_s, rows_t, sems):
            start = pl.multiple_of(where[0] * rows, rows)
            copies = [
                pltpu.make_async_copy(ref.at[pl.ds(start, rows)], to, sems.at[k])
                for k, (ref, to) in enumerate(((student, rows_s), (teacher, rows_t)))
            ]
            for copy in copies:
                copy.start()
            natural = lax.broadcasted_iota(jnp.int32, (width, width), 0)
            place = lax.broadcasted_iota(jnp.int32, (1, width), 1)
            source = place
            for k in range(fsdp):
                inside = (place >= k * depth) & (place < (k + 1) * depth)
                source = jnp.where(inside, place + (where[1 + k] - k) * depth, source)
            to_place[...] = jnp.where(natural == source, 1.0, 0.0).astype(LOW)
            copies[0].wait()
            x = kernel_nn(rows_s[...], to_place[...])
            x_low[...] = x.astype(LOW)
            entry[...] = soft_clip(x).astype(LOW)
            copies[1].wait()
            xt_low[...] = kernel_nn(rows_t[...], to_place[...]).astype(LOW)

        full = ((rows, width), LOW, whole(rows, width))
        have.x_low, have.entry, have.xt_low, have.leave = run.call(
            "place_rows",
            kernel,
            [
                (scalars, SCALARS),
                (student_in, IN_PLACE),
                (teacher_in, IN_PLACE),
            ],
            [full, full, full, ((width, width), LOW, whole(width, width))],
            scratch=[pltpu.VMEM((rows, width), LOW), pltpu.VMEM((rows, width), LOW), pltpu.SemaphoreType.DMA((2,))],
        )

    def prepare_slots():
        units = rows // 64
        first_unit = my_tensor * units

        def kernel(first, sizes, lengths, qid, kid, live_rows):
            for u in range(units):
                unit = first[0] + u
                slot = unit * 64
                size, length = sizes[unit], lengths[unit]
                begin = slot - lax.rem(slot, size)
                here = slice(u * 64, (u + 1) * 64)
                down = slot - begin + lax.broadcasted_iota(jnp.int32, (64, 128), 0)
                kid[here] = jnp.where(down < length, begin, -1)
                live_rows[here] = jnp.where(down < length, 1.0, 0.0)
                across = slot - begin + lax.broadcasted_iota(jnp.int32, (8, 64), 1)
                row = lax.broadcasted_iota(jnp.int32, (8, 64), 0)
                qid[:, here] = jnp.where(row == 0, begin, jnp.where(across < length, 1, 0))

        have.qid, have.kid, have.live_rows = run.call(
            "slots",
            kernel,
            [
                (first_unit.astype(jnp.int32).reshape(1), SCALARS),
                (bucket_size, SCALARS),
                (seq_length, SCALARS),
            ],
            [
                ((8, rows), jnp.int32, whole(8, rows)),
                ((rows, 128), jnp.int32, whole(rows, 128)),
                ((rows, 128), WIDE, whole(rows, 128)),
            ],
        )

    scale = HEAD_DIM ** (-0.5)

    def project_teacher():
        def work(product, refs, here):
            factor = jnp.where(pl.program_id(0) == 0, scale, 1.0)
            return [(product.astype(LOW) * factor.astype(LOW)).astype(LOW)]

        have.proj_t = times_weight(
            run, "project_teacher", have.xt_low, have.w_tqkv, narrow_tiles, work, [], [LOW]
        )[0]

    def project_student():
        def work(product, refs, here):
            factor = jnp.where(pl.program_id(0) == 0, scale, 1.0)
            return [((refs[0][0] * product).astype(LOW) * factor.astype(LOW)).astype(LOW)]

        have.proj_s = times_weight(
            run, "project_student", have.entry, have.w_qkv, narrow_tiles, work,
            [(have.betas, SCALARS)], [LOW],
        )[0]

    def attend(step):
        onto = [have.attended, have.t_attended, have.probs, have.gap] if step else []
        have.attended, have.t_attended, have.probs, have.gap = run_forward(
            run, step, 2, onto, have.qid, have.kid, have.proj_s, have.proj_t
        )

    square = ((rows, width), WIDE)
    square_low = ((rows, width), LOW)

    def close_teacher():
        def work(product, refs, outs, tile):
            here = rows_at(tile)
            normed, _ = norm_parts(refs[0][here].astype(WIDE) + product)
            outs[0][here] = normed
            outs[1][here] = normed.astype(LOW)

        have.t_first, have.t_first_low = times_turned(
            run, "close_teacher", have.t_attended, have.w_tqkv, [3], work,
            [], [have.xt_low], [square, square_low],
        )

    def close_student():
        def work(product, refs, outs, tile):
            betas, gain, x = refs
            here = rows_at(tile)
            normed, size = norm_parts(x[here].astype(WIDE) + betas[1] * product)
            outs[0][here] = normed
            outs[1][here] = jnp.broadcast_to(size, (TILE, 128))
            outs[2][here] = soft_clip(normed * gain[...]).astype(LOW)

        have.n_first, have.r_first, have.middle = times_turned(
            run, "close_student", have.attended, have.w_qkv, [3], work,
            [(have.betas, SCALARS), (have.first_gain, whole(1, width))],
            [have.x_low],
            [square, ((rows, 128), WIDE), square_low],
        )

    def up_teacher():
        def work(product, refs, here):
            return [(product * gelu_cdf(product)).astype(LOW)]

        have.t_hidden = times_weight(
            run, "up_teacher", have.t_first_low, have.w_up, wide_tiles(0), work, [], [LOW]
        )[0]

    def up_student():
        def work(product, refs, here):
            up = refs[0][2] * product
            cdf = gelu_cdf(up)
            return [(up * cdf).astype(LOW), (cdf + up * gelu_density(up)).astype(LOW)]

        have.hidden, have.slope = times_weight(
            run, "up_student", have.middle, have.w_up, wide_tiles(1), work,
            [(have.betas, SCALARS)], [LOW, LOW],
        )

    def down_teacher():
        def work(product, refs, outs, tile):
            here = rows_at(tile)
            normed, _ = norm_parts(refs[0][here] + product)
            outs[0][here] = normed
            put_turned(normed.astype(LOW), refs[1], outs[1], tile)

        have.t_result, have.t_leave = times_turned(
            run, "down_teacher", have.t_hidden, have.w_down, wide_tiles(0), work,
            [], [have.t_first, have.leave], [square, packed],
        )

    def down_student():
        def work(product, refs, outs, tile):
            betas, first_gain, second_gain, n_first, t_result, live_rows, leave = refs
            here = rows_at(tile)
            normed, size = norm_parts(n_first[here] * first_gain[...] + betas[3] * product)
            result = normed * second_gain[...]
            d_result = jnp.where(live_rows[here][:, 0:1] > 0, result - t_result[here], 0.0)
            add_column_sums(outs[2], d_result * normed, tile)
            d_second = norm_back(d_result * second_gain[...], normed, size)
            outs[0][here] = d_second
            outs[1][here] = (betas[3] * d_second).astype(LOW)
            put_turned(result.astype(LOW), leave, outs[3], tile)

        have.d_second, have.grad_z, have.sums_second, have.s_leave = times_turned(
            run, "down_student", have.hidden, have.w_down, wide_tiles(1), work,
            [
                (have.betas, SCALARS),
                (have.first_gain, whole(1, width)),
                (have.second_gain, whole(1, width)),
            ],
            [have.n_first, have.t_result, have.live_rows, have.leave],
            [square, square_low, ((8, width), WIDE), packed],
        )


    def split_one(a, b):
        return tuple(value.reshape(depth, tensor // 2, -1).transpose(1, 0, 2) for value in (a, b))

    def split_qkv(a, b):
        value = jnp.concatenate([a, b], axis=1).reshape(depth, 3, tensor, part).transpose(2, 0, 1, 3)
        value = value.reshape(tensor, depth, 3 * part)
        return value[: tensor // 2], value[tensor // 2 :]

    def share_down():
        return Task(scatter_weight(run, "g_down", have.grad_z, have.hidden, None, keep("grad_down")))

    def back_down():
        def work(product, refs, here):
            return [(refs[0][2] * (product * refs[1][here].astype(WIDE))).astype(LOW)]

        have.grad_u = times_weight(
            run, "back_down", have.grad_z, have.w_down, wide_tiles(1), work,
            [(have.betas, SCALARS), (have.slope, pl.BlockSpec((rows, width), lambda j: (0, j)))],
            [LOW],
        )[0]

    def share_up():
        return Task(scatter_weight(run, "g_up", have.middle, have.grad_u, None, keep("grad_up"), swaps=True))

    def back_up():
        def work(product, refs, outs, tile):
            betas, gain, d_second, n_first, r_first, w_out = refs
            here = rows_at(tile)
            normed = n_first[here]
            d_h = d_second[here] + product * clip_slope(normed * gain[...])
            add_column_sums(outs[3], d_h * normed, tile)
            d_first = norm_back(d_h * gain[...], normed, r_first[here][:, 0:1])
            outs[0][here] = d_first
            grad_o = (betas[1] * d_first).astype(LOW)
            outs[1][here] = grad_o
            outs[2][here] = kernel_nn(grad_o, w_out[...]).astype(LOW)

        have.d_first, have.grad_o, have.d_attended, have.sums_first = times_turned(
            run, "back_up", have.grad_u, have.w_up, wide_tiles(1), work,
            [(have.betas, SCALARS), (have.first_gain, whole(1, width))],
            [have.d_second, have.n_first, have.r_first, (have.w_qkv, 3 * width)],
            [square, square_low, square_low, ((8, width), WIDE)],
        )

    def share_out():
        beside = (have.sums_first, have.sums_second)
        return Task(
            scatter_weight(run, "g_out", have.grad_o, have.attended, split_one, keep("grad_out"), beside)
        )

    def back_attend():
        have.g_all = run_backward(
            run, have.betas, have.proj_s, have.d_attended, have.probs, have.gap
        )

    def share_qkv():
        return Task(scatter_weight(run, "g_qkv", have.entry, have.g_all, split_qkv, keep("grad_qkv")))

    def back_entry():
        def work(product, refs, outs, tile):
            here = rows_at(tile)
            x = refs[1][here].astype(WIDE)
            put_turned((refs[0][here] + product * clip_slope(x)).astype(LOW), refs[2], outs[0], tile)

        have.g_leave = times_turned(
            run, "back_entry", have.g_all, have.w_qkv, narrow_tiles, work,
            [], [have.d_first, have.x_low, have.leave], [packed],
        )[0]

    def bring(name, shard, finish_rows):
        return Task(gather_weight(run, name, shard, finish_rows, keep(name)))

    ta = bring("w_tqkv", shard_tqkv, finish_qkv)
    sa = bring("w_qkv", shard_qkv, finish_qkv)
    c = bring("w_up", shard_up, None)
    d = bring("w_down", shard_down, None)
    go_on(ta)
    run.wait(run.shards[0])
    small = Task(gather_small(gains, magnitudes(), small_store))
    go_on(sa)
    go_on(small)
    run.land(small)
    prepare_slots()
    go_on(small)
    run.land(small)
    go_on(ta)
    go_on(small)
    prepare()
    run.land(small)
    go_on(sa)
    go_on(ta)
    run.land(sa)
    go_on(c)
    go_on(d)
    run.land(ta, only=0)
    go_on(sa)
    go_on(small)
    run.land(ta, only=1)
    run.land(small)
    run.fence()
    go_on(ta)
    go_on(small)
    run.land(sa, small)
    run.fence()
    finish(small)
    finish(ta)
    go_on(sa)
    go_on(c)
    project_teacher()
    finish(sa)
    project_student()
    attend(0)
    run.land(c, d)
    run.fence()
    go_on(c)
    attend(1)
    go_on(d)
    close_teacher()
    run.land(c)
    close_student()
    finish(c)
    run.land(d, only=0)
    up_teacher()
    up_student()
    run.land(d, only=1)
    run.fence()
    finish(d)
    down_teacher()
    t_leave = Task(leave_columns(run, "arrive_teacher", have.t_leave, LOW, keep("teacher_out")))
    go_on(t_leave)
    down_student()
    s_leave = Task(leave_columns(run, "arrive_student", have.s_leave, LOW, keep("student_out")))
    down = share_down()
    go_on(down)
    back_down()
    run.land(t_leave)
    up = share_up()
    go_on(up)
    go_on(s_leave)
    go_on(down)
    go_on(up)
    back_up()
    run.land(s_leave)
    back_attend()
    go_on(down)
    qkv = share_qkv()
    go_on(qkv)
    go_on(up)
    back_entry()
    g_leave = Task(leave_columns(run, "arrive_grad", have.g_leave, WIDE, keep("input_grad")))
    go_on(g_leave)
    go_on(qkv)
    go_on(down)
    go_on(up)
    out = share_out()
    go_on(out)
    finish(t_leave)
    run.land(qkv)
    go_on(out)
    go_on(qkv)
    run.land(up)
    finish(s_leave)
    go_on(up)
    go_on(out)
    run.land(qkv, down)
    finish(g_leave)
    go_on(qkv)
    go_on(out)
    finish(qkv)
    finish(out)
    finish(up)
    finish(down)

    def inside(grad, latent):
        return jnp.where(jnp.abs(latent) <= 1.0, grad, 0.0)

    return (
        have.student_out,
        have.teacher_out,
        have.input_grad,
        inside(have.grad_qkv.reshape(depth, 3, part).transpose(1, 0, 2), qkv_latent),
        inside(have.grad_out[:, :part].T, out_latent),
        inside(have.grad_up, up_latent),
        inside(have.grad_down.T, down_latent),
        have.grad_out[:, part],
        have.grad_out[:, part + 1],
    )


def solution(mesh):
    placed = (
        P(FSDP, None),
        P(FSDP, None),
        P(FSDP),
        P(FSDP),
        P(None, FSDP, TENSOR),
        P(TENSOR, FSDP),
        P(FSDP, TENSOR),
        P(TENSOR, FSDP),
        P(FSDP),
        P(FSDP),
        P(None, FSDP, TENSOR),
        P(TENSOR, FSDP),
        P(FSDP, TENSOR),
        P(TENSOR, FSDP),
    )
    return jax.shard_map(
        body,
        mesh=mesh,
        in_specs=placed,
        out_specs=(
            P(FSDP, TENSOR),
            P(FSDP, TENSOR),
            P(FSDP, TENSOR),
            P(None, FSDP, TENSOR),
            P(TENSOR, FSDP),
            P(FSDP, TENSOR),
            P(TENSOR, FSDP),
            P(FSDP),
            P(FSDP),
        ),
        check_vma=False,
    )
```

```python
import functools
import math
import types

import jax
import jax.numpy as jnp
from jax import lax
from jax.experimental import pallas as pl
from jax.experimental.pallas import tpu as pltpu
from jax.sharding import PartitionSpec as P

HEAD_DIM = 64
PAIR = 2 * HEAD_DIM
TILE = 256
CLIP_RANGE = 2.5
ATT_WEIGHT = 0.015625
EPSILON = 1e-06
NEG_FILL = -1000000000.0
LOW = jnp.bfloat16
WIDE = jnp.float32
FSDP = "fsdp"
TENSOR = "tensor"
VMEM_BYTES = 60 * 1024 * 1024
WEIGH = 5


IN_PLACE = pl.BlockSpec(memory_space=pl.ANY)
SCALARS = pl.BlockSpec(memory_space=pltpu.SMEM)


class Task:
    def __init__(self, stages):
        self.stages = stages
        self.arrays = None

    def go_on(self):
        try:
            got = next(self.stages) if self.arrays is None else self.stages.send(self.arrays)
            self.arrays = list(got)
        except StopIteration:
            self.arrays = ()

    def finish(self):
        while self.arrays != ():
            self.go_on()


class Order:
    def __init__(self):
        self.after = []
        self.landing = []
        self.shards = []

    def land(self, *tasks, only=None):
        for task in tasks:
            for k in range(len(task.arrays)):
                if only is None or only == k:
                    self.landing.append((task, k))

    def wait(self, *arrays):
        self.after = self.after + list(arrays)

    def fence(self):
        def kernel(out):
            out[...] = jnp.zeros((8, 128), WIDE)

        self.call("fence", kernel, [], [((8, 128), WIDE, whole(8, 128))])

    def call(self, name, kernel, ins, outs, grid=(1,), scratch=(), flops=0, moved=0, onto=()):
        waits = [value for value in self.after if not any(value is array for array in onto)]
        passed = [task.arrays[k] for task, k in self.landing]
        count, given = len(ins), len(outs)
        skip = len(onto) + len(passed) + len(waits)

        def wrapped(*refs):
            kernel(*refs[:count], *refs[count + skip : count + skip + given], *refs[count + skip + given + len(passed) :])

        aliases = {count + k: k for k in range(len(onto))}
        aliases.update({count + len(onto) + k: given + k for k in range(len(passed))})
        results = pl.pallas_call(
            wrapped,
            grid=grid,
            in_specs=[spec for _, spec in ins] + [IN_PLACE] * skip,
            out_specs=[spec for _, _, spec in outs] + [IN_PLACE] * len(passed),
            out_shape=[jax.ShapeDtypeStruct(shape, dtype) for shape, dtype, _ in outs]
            + [jax.ShapeDtypeStruct(array.shape, array.dtype) for array in passed],
            scratch_shapes=list(scratch),
            input_output_aliases=aliases,
            compiler_params=pltpu.CompilerParams(vmem_limit_bytes=VMEM_BYTES),
            cost_estimate=pl.CostEstimate(flops=flops * WEIGH, bytes_accessed=moved * WEIGH, transcendentals=0),
            name=name,
        )(*[array for array, _ in ins], *onto, *passed, *waits)
        rest = list(results[given:])
        for task, k in self.landing:
            task.arrays[k] = rest.pop(0)
        self.landing = []
        self.after = [results[0]]
        return list(results[:given])


def whole(*shape):
    return pl.BlockSpec(shape, lambda *_: (0,) * len(shape))


def swap(value, axis, bit):
    size = lax.axis_size(axis)
    return lax.ppermute(value, axis, [(i, i ^ bit) for i in range(size)])


def swap_first(value):
    return lax.ppermute(value, FSDP, [(i, i ^ (4 if i % 2 else 2)) for i in range(8)])


def swap_second(value):
    return lax.ppermute(value, FSDP, [(i, i ^ (2 if i % 2 else 4)) for i in range(8)])


def bits_of(axis):
    size = lax.axis_size(axis)
    bits = [1 << k for k in range(size.bit_length() - 1)]
    return [bits[0]] + bits[:0:-1] if bits else []


def order_of(axis):
    order = [0]
    for bit in reversed(bits_of(axis)):
        order = order + [o ^ bit for o in order]
    return order


def two_links(rows):
    return lax.axis_size(FSDP) == 8 and rows % 32 == 0


CHIP_ORDERS = ([0, 2, 4, 6, 1, 5, 3, 7], [0, 4, 2, 6, 1, 3, 5, 7])


def feature_order(depth):
    if not two_links(depth):
        return jnp.array(order_of(FSDP), jnp.int32)
    odd = lax.axis_index(FSDP) & 1
    return jnp.where(odd > 0, jnp.array(CHIP_ORDERS[1], jnp.int32), jnp.array(CHIP_ORDERS[0], jnp.int32))


def reorder(blocks, back):
    plain = order_of(FSDP)
    results = []
    for chip in CHIP_ORDERS:
        if back:
            results.append([blocks[chip.index(m)] for m in plain])
        else:
            results.append([blocks[plain.index(m)] for m in chip])
    odd = lax.axis_index(FSDP) & 1
    return [jnp.where(odd > 0, two, one) for one, two in zip(*results)]


def join_columns(run, name, arrays, moves, columns):
    rows = arrays[0].shape[0]

    def kernel(*refs):
        for k, source, target, count in moves:
            refs[-1][:, target : target + count] = refs[k][:, source : source + count]

    return run.call(
        name,
        kernel,
        [(array, whole(*array.shape)) for array in arrays],
        [((rows, columns), LOW, whole(rows, columns))],
        moved=4 * rows * columns,
    )[0]


def side_by_side(run, name, left, right):
    n = left.shape[1]
    return join_columns(run, name, [left, right], [(0, 0, 0, n), (1, 0, n, n)], 2 * n)


def rows_side_by_side(run, name, value, rows):
    total, n = value.shape
    count = total // rows

    def kernel(ref, out):
        for k in range(count):
            out[:, k * n : (k + 1) * n] = ref[k * rows : (k + 1) * rows]

    return run.call(
        name, kernel, [(value, whole(total, n))], [((rows, count * n), LOW, whole(rows, count * n))], moved=4 * total * n
    )[0]


def gather_weight(run, name, shard, finish, store):
    value = shard()
    run.shards.append(value)
    if finish is None:
        (got,) = yield [lax.all_gather(value, TENSOR, axis=0, tiled=True)]
        mine = rows_side_by_side(run, name + "_rows", got, value.shape[0])
    else:
        (got,) = yield [swap(value, TENSOR, 2)]
        value = side_by_side(run, name + "_join", value, got)
        (got,) = yield [swap(value, TENSOR, 1)]
        mine = finish(name + "_rows", value, got)
    if two_links(mine.shape[0]):
        sibling, first = yield [swap(mine, FSDP, 1), swap_first(mine)]
        first, first_other = yield [first, swap_first(sibling)]
        second_other, second = yield [swap(first, FSDP, 1), swap(first_other, FSDP, 1)]
        (both,) = yield [swap_first(second)]
        both_other = swap(both, FSDP, 1)
        store((mine, first, second, both, sibling, second_other, first_other, both_other))
    else:
        for bit in reversed(bits_of(FSDP)):
            mine = jnp.concatenate([mine, swap(mine, FSDP, bit)], axis=0)
        store((mine,))


def add_low(left, right):
    return (left.astype(WIDE) + right.astype(WIDE)).astype(LOW)


def scatter_weight(run, name, left, right, split, store, beside=None, triple=False):
    rows, width = left.shape
    fsdp = lax.axis_size(FSDP)
    depth = width // fsdp
    columns = right.shape[1]
    middle, half = width // 2, columns // 2
    step = half
    steps = half // step
    side = pl.BlockSpec((rows, step), lambda j: (0, j))
    cost = dict(flops=2 * rows * middle * columns, moved=2 * (rows * columns + 2 * middle * columns))
    added = []
    out_step = step
    if beside is not None:
        added = [(value, whole(8, width)) for value in beside]
        lanes = step // 2
        out_step = 2 * (lanes + 64)
        half = steps * out_step
        columns = 2 * half

    def product(left_ref, right_ref, sums, start):
        value = kernel_tn(left_ref[...], right_ref[...])
        if not sums:
            return value
        turned = [
            jnp.broadcast_to(jnp.sum(ref[:, start : start + middle], axis=0, keepdims=True), (128, middle)).T for ref in sums
        ]
        lane = lax.broadcasted_iota(jnp.int32, (middle, 128), 1)
        more = jnp.where(lane == 0, turned[0], jnp.where(lane == 1, turned[1], 0.0))[:, :64]
        return jnp.concatenate([value[:, :lanes], more, value[:, lanes:], more], axis=1)

    def far_kernel(left_ref, right_ref, *refs):
        refs[-1][...] = product(left_ref, right_ref, refs[:-1], middle).astype(LOW)

    far = run.call(
        name + "_far",
        far_kernel,
        [(left, pl.BlockSpec((rows, middle), lambda j: (0, 1))), (right, side)] + added,
        [((middle, columns), LOW, pl.BlockSpec((middle, out_step), lambda j: (0, j)))],
        grid=(2 * steps,),
        **cost,
    )[0]
    (got,) = yield [swap(far, FSDP, 1)]
    near_ins = [
        (left, pl.BlockSpec((rows, middle), lambda j: (0, 0))),
        (right, side),
        (got, pl.BlockSpec((middle, out_step), lambda j: (0, j))),
    ] + added
    if two_links(depth):
        one = ((depth, columns), LOW, whole(depth, columns))
        at = [slice(k * depth, (k + 1) * depth) for k in range(4)]

        def near_kernel(left_ref, right_ref, got_ref, *refs):
            keep, send = refs[-2:]
            total = (product(left_ref, right_ref, refs[:-2], 0) + got_ref[...].astype(WIDE)).astype(LOW)
            keep[at[0]], keep[at[1]] = total[at[0]], total[at[2]]
            send[at[0]], send[at[1]] = total[at[1]], total[at[3]]

        def second(keep, got, own, onward):
            own[...] = add_low(keep[at[0]], got[at[0]])
            onward[...] = add_low(keep[at[1]], got[at[1]])

        def third(own, got, *outs):
            n = columns // len(outs)
            for k, out in enumerate(outs):
                lanes = slice(k * n, (k + 1) * n)
                out[...] = add_low(own[:, lanes], got[:, lanes])

        def third_split(own, got, keep, send):
            n = columns // 12
            for p in range(4):
                out = keep if p < 2 else send
                for k in range(3):
                    lanes = slice((4 * k + p) * n, (4 * k + p + 1) * n)
                    out[at[p % 2], k * n : (k + 1) * n] = add_low(own[:, lanes], got[:, lanes])

        def third_rows(where, own, got, keep, send):
            n = columns // 4
            for k in range(4):
                lanes = slice(k * n, (k + 1) * n)
                row = pl.multiple_of((where[k] & 1) * depth, depth)

                @pl.when(where[k] < 2)
                def _():
                    keep[pl.ds(row, depth)] = add_low(own[:, lanes], got[:, lanes])

                @pl.when(where[k] >= 2)
                def _():
                    send[pl.ds(row, depth)] = add_low(own[:, lanes], got[:, lanes])

        pair = ((2 * depth, columns), LOW, pl.BlockSpec((2 * depth, out_step), lambda j: (0, j)))
        keep, send = run.call(name + "_near", near_kernel, near_ins, [pair] * 2, grid=(2 * steps,), **cost)
        (got,) = yield [swap_first(send)]
        full = whole(2 * depth, columns)
        own, onward = run.call(name + "_add2", second, [(keep, full), (got, full)], [one] * 2, moved=6 * depth * columns)
        (got,) = yield [swap_second(onward)]
        ins = [(own, one[2]), (got, one[2])]
        if split is None:
            shape = (2 * depth, columns // 4)
            m = jnp.arange(4, dtype=jnp.int32) ^ lax.axis_index(TENSOR)
            ins = [((m & 1) * 2 + (m >> 1), SCALARS)] + ins
            here = run.call(
                name + "_add3", third_rows, ins, [(shape, LOW, whole(*shape))] * 2, moved=6 * depth * columns
            )
            split = lambda *parts: tuple(value.reshape(2, depth, -1) for value in parts)
        else:
            shape = (2 * depth, columns // 4) if triple else (depth, half)
            work = third_split if triple else third
            here = run.call(name + "_add3", work, ins, [(shape, LOW, whole(*shape))] * 2, moved=6 * depth * columns)
            if triple:
                split = lambda *parts: tuple(value.reshape(2, depth, -1) for value in parts)
    else:

        def near_kernel(left_ref, right_ref, got_ref, *refs):
            value = product(left_ref, right_ref, refs[:-1], 0)
            refs[-1][...] = (value + got_ref[...].astype(WIDE)).astype(LOW)

        here = run.call(
            name + "_near",
            near_kernel,
            near_ins,
            [((middle, columns), LOW, pl.BlockSpec((middle, out_step), lambda j: (0, j)))],
            grid=(2 * steps,),
            **cost,
        )[0].reshape(fsdp // 2, depth, columns)
        count = fsdp // 2
        for bit in bits_of(FSDP)[1:]:
            count //= 2
            (got,) = yield [swap(here[count:], FSDP, bit)]
            here = add_low(here[:count], got)
        if split is None:
            here = here[0].reshape(depth, 4, -1).transpose(1, 0, 2).reshape(4 * depth, -1)
        else:
            here = (here[0, :, :half], here[0, :, half:])
    if split is None:
        (here,) = yield [lax.psum_scatter(here, TENSOR, scatter_dimension=0, tiled=True)]
        store(here.astype(WIDE))
        return
    keep, send = split(*here)
    for bit in bits_of(TENSOR):
        (got,) = yield [swap(send, TENSOR, bit)]
        total = add_low(keep, got)
        keep, send = total[: total.shape[0] // 2], total[total.shape[0] // 2 :]
    store(total[0].astype(WIDE))


def gather_small(gains, sums, store):
    depth = gains.shape[1]
    block = jnp.concatenate([sums, jnp.pad(gains, ((0, 6), (0, 128 - depth)))], axis=0)[None]
    for bit in reversed(bits_of(FSDP)):
        (got,) = yield [swap(block, FSDP, bit)]
        block = jnp.concatenate([block, got], axis=0)
    parts = [block[k, 8:10, :depth] for k in range(block.shape[0])]
    gains = jnp.concatenate(reorder(parts, False) if two_links(depth) else parts, axis=1)
    sums = block[:, :8]
    while sums.shape[0] > 1:
        sums = sums[: sums.shape[0] // 2] + sums[sums.shape[0] // 2 :]
    sums = sums[0]
    for bit in bits_of(TENSOR):
        (got,) = yield [swap(sums, TENSOR, bit)]
        sums = sums + got
    store(gains, sums[0])


def leave_columns(run, name, value, dtype, count, store):
    size = lax.axis_size(TENSOR)
    (got,) = yield [lax.all_to_all(value, TENSOR, 0, 0, tiled=True)]
    columns, rows = got.shape[0] // size, got.shape[1] // count

    def kernel(ref, *outs):
        for k, out in enumerate(outs):
            out[...] = ref[:, k * rows : (k + 1) * rows].astype(dtype)

    results = run.call(
        name,
        kernel,
        [(got, pl.BlockSpec((columns, count * rows), lambda i: (i, 0)))],
        [((columns, size * rows), dtype, pl.BlockSpec((columns, rows), lambda i: (0, i)))] * count,
        grid=(size,),
        moved=8 * columns * rows,
    )
    store(*[result.T for result in results])


def put_turned(value, natural, out, tile):
    out[:, tile * TILE : (tile + 1) * TILE] = kernel_nt(natural[...], value).astype(LOW)


def dot(left, right):
    return jnp.dot(left, right, preferred_element_type=WIDE)


def dot_tn(left, right):
    return lax.dot_general(left, right, (((0,), (0,)), ((), ())), preferred_element_type=WIDE)


def dot_nt(left, right):
    return lax.dot_general(left, right, (((1,), (1,)), ((), ())), preferred_element_type=WIDE)


def soft_clip(value):
    return CLIP_RANGE * jnp.tanh(value / CLIP_RANGE)


def clip_slope(value):
    bent = jnp.tanh(value / CLIP_RANGE)
    return 1.0 - bent * bent


def norm_parts(value):
    centre = value - jnp.mean(value, axis=-1, keepdims=True)
    scale = lax.rsqrt(jnp.mean(centre * centre, axis=-1, keepdims=True) + EPSILON)
    return centre * scale, scale


def norm_back(grad, normed, scale):
    return scale * (
        grad
        - jnp.mean(grad, axis=-1, keepdims=True)
        - normed * jnp.mean(grad * normed, axis=-1, keepdims=True)
    )


def gelu_cdf(value):
    return 0.5 + 0.5 * lax.erf(value * math.sqrt(0.5))


def gelu_density(value):
    return jnp.exp(-0.5 * value * value) * (1.0 / math.sqrt(2.0 * math.pi))


def kernel_nt(left, right):
    return lax.dot_general(left, right, (((1,), (1,)), ((), ())), preferred_element_type=WIDE)


def kernel_tn(left, right):
    return lax.dot_general(left, right, (((0,), (0,)), ((), ())), preferred_element_type=WIDE)


def kernel_nn(left, right):
    return jnp.dot(left, right, preferred_element_type=WIDE)


def times_weight(run, name, left, parts, tiles, work, extras, outs):
    rows, width = left.shape
    base, stride = tiles[0], tiles[1] - tiles[0]
    count = len(parts)

    def kernel(*refs):
        weight = refs[-1]
        row = 0
        for block in refs[1 : 1 + count]:
            weight[pl.ds(row, block.shape[0])] = block[...]
            row += block.shape[0]
        for r in range(0, rows, TILE):
            here = pl.ds(r, TILE)
            values = work(kernel_nn(refs[0][here], weight[...]), refs[1 + count : 1 + count + len(extras)], here)
            for ref, value in zip(refs[1 + count + len(extras) : -1], values):
                ref[here] = value

    columns = width * len(tiles)
    return run.call(
        name,
        kernel,
        [(left, whole(rows, width))]
        + [(part, pl.BlockSpec((part.shape[0], width), lambda j: (0, base + stride * j))) for part in parts]
        + extras,
        [((rows, columns), dtype, pl.BlockSpec((rows, width), lambda j: (0, j))) for dtype in outs],
        grid=(len(tiles),),
        scratch=[pltpu.VMEM((width, width), LOW)],
        flops=2 * rows * width * columns,
        moved=2 * (rows * width + width * columns + len(outs) * rows * columns),
    )


def times_turned(run, name, left, parts, tiles, work, extras, late, outs):
    rows, wide = left.shape
    width = sum(part.shape[0] for part in parts)
    step = wide // len(tiles)
    base, stride = tiles[0], tiles[1] - tiles[0] if len(tiles) > 1 else 1
    count, more = len(parts), len(extras)
    sources, held = [], []
    for item in late:
        pieces, column = item if isinstance(item, tuple) else ([item], 0)
        columns = pieces[0].shape[1] if column == 0 and not isinstance(item, tuple) else width
        row = 0
        for piece in pieces:
            sources.append((piece, len(held), row, column, columns))
            row += piece.shape[0]
        held.append(pltpu.VMEM((row, columns), pieces[0].dtype))
    first_late = 1 + count + more
    first_out = first_late + len(sources)
    first_held = first_out + len(outs) + 2

    def kernel(*refs):
        total, weight = refs[first_out + len(outs)], refs[first_out + len(outs) + 1]
        scratch, sems = refs[first_held:-1], refs[-1]
        j = pl.program_id(0)
        copies = []
        for k, (piece, to, row, column, columns) in enumerate(sources):
            copies.append(
                pltpu.make_async_copy(
                    refs[first_late + k].at[:, pl.ds(column, columns)],
                    scratch[to].at[pl.ds(row, piece.shape[0])],
                    sems.at[k],
                )
            )

        @pl.when(j == 0)
        def _():
            for copy in copies:
                copy.start()

        row = 0
        for block in refs[1 : 1 + count]:
            weight[pl.ds(row, block.shape[0])] = block[...]
            row += block.shape[0]
        product = kernel_nt(refs[0][...], weight[...])

        @pl.when(j == 0)
        def _():
            total[...] = product

        @pl.when(j > 0)
        def _():
            total[...] = total[...] + product

        @pl.when(j == len(tiles) - 1)
        def _():
            for copy in copies:
                copy.wait()
            for tile in range(rows // TILE):
                work(
                    total[pl.ds(tile * TILE, TILE)],
                    list(refs[1 + count : first_late]) + list(scratch),
                    refs[first_out : first_out + len(outs)],
                    tile,
                )

    return run.call(
        name,
        kernel,
        [(left, pl.BlockSpec((rows, step), lambda j: (0, j)))]
        + [(part, pl.BlockSpec((part.shape[0], step), lambda j: (0, base + stride * j))) for part in parts]
        + extras
        + [(piece, IN_PLACE) for piece, _, _, _, _ in sources],
        [(shape, dtype, whole(*shape)) for shape, dtype in outs],
        grid=(len(tiles),),
        scratch=[pltpu.VMEM((rows, width), WIDE), pltpu.VMEM((width, step), LOW)]
        + held
        + [pltpu.SemaphoreType.DMA((max(len(sources), 1),))],
        flops=2 * rows * width * wide,
        moved=2 * (rows * wide + width * wide),
    )


def rows_at(tile):
    return pl.ds(tile * TILE, TILE)


def tile_rows(columns):
    return pl.BlockSpec((TILE, columns), lambda i: (i, 0))


def add_column_sums(ref, value, tile):
    total = jnp.sum(value.reshape(value.shape[0] // 8, 8, value.shape[1]), axis=0)
    ref[...] = total if tile == 0 else ref[...] + total


def both_heads(value):
    first = lax.broadcasted_iota(jnp.int32, (1, PAIR), 1) < HEAD_DIM
    zero = jnp.zeros((), value.dtype)
    return jnp.concatenate([jnp.where(first, value, zero), jnp.where(first, zero, value)], axis=0)


def own_heads(value):
    return jnp.concatenate([value[:HEAD_DIM, :TILE], value[HEAD_DIM:, TILE:]], axis=0).T


def attend_forward(qid, kid, qs, ks, vs, qt, kt, vt, os, ot, probs_out, gap_out):
    keep = kid[:, 0:1] == qid[0:1, :]
    both = keep & (qid[1:2, :] > 0)
    bias = jnp.where(keep, 0.0, NEG_FILL)
    bias = jnp.concatenate([bias, bias], axis=1)
    seen = jnp.where(both, 1.0, 0.0)
    seen = jnp.concatenate([seen, seen], axis=1)

    def soft(score):
        masked = score + bias
        expo = jnp.exp(masked - jnp.max(masked, axis=0, keepdims=True))
        return (expo * (1.0 / jnp.sum(expo, axis=0, keepdims=True))).astype(LOW)

    for p in range(qs.shape[1] // PAIR):
        here = slice(p * PAIR, (p + 1) * PAIR)
        score_s = kernel_nt(ks[:, here], both_heads(qs[:, here]))
        score_t = kernel_nt(kt[:, here], both_heads(qt[:, here]))
        gap_out[0, p] = ((score_s - score_t) * seen).astype(LOW)
        probs = soft(score_s)
        probs_out[0, p] = probs
        os[:, here] = own_heads(kernel_tn(vs[:, here], probs)).astype(LOW)
        ot[:, here] = own_heads(kernel_tn(vt[:, here], soft(score_t))).astype(LOW)


def attend_backward(betas, proj, grad, probs, gap, out):
    width = grad.shape[1]
    up = jnp.asarray(1.0 / ATT_WEIGHT, LOW)
    b = betas[0] * ATT_WEIGHT
    scale = HEAD_DIM ** (-0.5)
    for p in range(width // PAIR):
        at_q = slice(p * PAIR, (p + 1) * PAIR)
        at_k = slice(width + p * PAIR, width + (p + 1) * PAIR)
        at_v = slice(2 * width + p * PAIR, 2 * width + (p + 1) * PAIR)
        grad_two = both_heads(grad[:, at_q] * up)
        prob_low = probs[0, p]
        prob = prob_low.astype(WIDE)
        weighted = prob * kernel_nt(proj[:, at_v], grad_two)
        inner = jnp.sum(weighted, axis=0, keepdims=True)
        d_score = (weighted - prob * inner + gap[0, p].astype(WIDE)).astype(LOW)
        out[:, at_v] = (b * kernel_nn(prob_low, grad_two)).astype(LOW)
        out[:, at_k] = (b * kernel_nn(d_score, both_heads(proj[:, at_q]))).astype(LOW)
        out[:, at_q] = own_heads((b * scale) * kernel_tn(proj[:, at_k], d_score)).astype(LOW)


def run_forward(run, step, steps, onto, qid, kid, proj_s, proj_t):
    rows, wide = proj_s.shape
    width = wide // 3
    pairs = width // PAIR
    tiles = rows // TILE

    def part(j):
        return pl.BlockSpec((TILE, width // steps), lambda b: (b, j * steps + step))

    square = pl.BlockSpec((1, pairs // steps, TILE, 2 * TILE), lambda b: (b, step, 0, 0))
    return run.call(
        "attend_forward",
        attend_forward,
        [(qid, pl.BlockSpec((8, TILE), lambda b: (0, b))), (kid, pl.BlockSpec((TILE, 128), lambda b: (b, 0)))]
        + [(value, part(j)) for value in (proj_s, proj_t) for j in range(3)],
        [((rows, width), LOW, part(0))] * 2 + [((tiles, pairs, TILE, 2 * TILE), LOW, square)] * 2,
        grid=(tiles,),
        flops=32 * rows * TILE * width // steps,
        moved=8 * rows * wide // steps,
        onto=onto,
    )


def run_backward(run, betas, proj_s, grad, probs, gap):
    rows, wide = proj_s.shape
    width = wide // 3
    pairs = width // PAIR
    square = pl.BlockSpec((1, pairs, TILE, 2 * TILE), lambda b: (b, 0, 0, 0))
    return run.call(
        "attend_backward",
        attend_backward,
        [(betas, SCALARS), (proj_s, tile_rows(wide)), (grad, tile_rows(width)), (probs, square), (gap, square)],
        [((rows, wide), LOW, tile_rows(wide))],
        grid=(rows // TILE,),
        flops=16 * rows * TILE * width,
        moved=8 * rows * wide,
    )[0]


def body(
    student_in,
    teacher_in,
    bucket_size,
    seq_length,
    qkv_latent,
    out_latent,
    up_latent,
    down_latent,
    gain_attn,
    gain_ffn,
    teach_qkv,
    teach_out,
    teach_up,
    teach_down,
):
    width = student_in.shape[1]
    fsdp = lax.axis_size(FSDP)
    tensor = lax.axis_size(TENSOR)
    rows = student_in.shape[0] // tensor
    depth = width // fsdp
    hidden_width = up_latent.shape[1] * tensor
    my_fsdp = lax.axis_index(FSDP)
    my_tensor = lax.axis_index(TENSOR)
    first_row = my_tensor * rows
    order = feature_order(depth)
    order_t = order_of(TENSOR)

    have = types.SimpleNamespace()
    run = Order()

    def keep(*names):
        def store(*values):
            for name, value in zip(names, values):
                setattr(have, name, value)

        return store

    def go_on(*tasks):
        for task in tasks:
            task.go_on()

    def finish(*tasks):
        for task in tasks:
            task.finish()

    gains = jnp.stack([gain_attn, gain_ffn]).astype(WIDE)

    def magnitudes():
        latents = (qkv_latent.reshape(-1, qkv_latent.shape[2]), out_latent, up_latent, down_latent)

        def kernel(*refs):
            lane = lax.broadcasted_iota(jnp.int32, (8, 128), 1)
            total = jnp.zeros((8, 128), WIDE)
            for k in range(4):
                total = jnp.where(lane == k, jnp.sum(jnp.abs(refs[k][...])), total)
            refs[4][...] = total

        return run.call(
            "magnitudes", kernel, [(value, whole(*value.shape)) for value in latents], [((8, 128), WIDE, whole(8, 128))]
        )[0]

    def pack_qkv(value):
        return value.astype(LOW).transpose(1, 0, 2).reshape(depth, -1)

    part = width // tensor

    def finish_qkv(name, near, far):
        moves = []
        for p in range(tensor):
            for k in range(4):
                moves.append((p // 2, (p % 2) * 4 * part + k * part, k * width + p * part, part))
        return join_columns(run, name, [near, far], moves, 4 * width)

    narrow_tiles = [0, 1, 2]

    def wide_tiles(which):
        return [2 * p + which for p in range(tensor)]

    def signs(value):
        return jnp.sign(value).astype(LOW)


    def shard_tqkv():
        return jnp.concatenate([pack_qkv(teach_qkv), teach_out.T], axis=1)

    def shard_qkv():
        return jnp.concatenate([pack_qkv(signs(qkv_latent)), signs(out_latent).T], axis=1)

    def pack_signs(name, teach, latent):
        def kernel(teach_ref, latent_ref, out):
            value = latent_ref[...]
            n = value.shape[1]
            out[:, :n] = teach_ref[...]
            out[:, n:] = jnp.where(value > 0, 1.0, jnp.where(value < 0, -1.0, 0.0)).astype(LOW)

        r, n = teach.shape
        return run.call(
            name, kernel, [(teach, whole(r, n)), (latent, whole(r, n))], [((r, 2 * n), LOW, whole(r, 2 * n))]
        )[0]

    def shard_up():
        return pack_signs("pack_up", teach_up, up_latent)

    def shard_down():
        return pack_signs("pack_down", teach_down.T, down_latent.T)

    def small_store(all_gains, totals):
        have.first_gain = all_gains[0:1]
        have.second_gain = all_gains[1:2]
        factors = (
            2.0 / (3 * width * width) / math.sqrt(width),
            2.0 / (width * width) / math.sqrt(width),
            2.0 / (width * hidden_width) / math.sqrt(width),
            2.0 / (width * hidden_width) / math.sqrt(hidden_width),
        )
        have.betas = totals[:4] * jnp.array(factors, WIDE)

    packed = ((width, rows), LOW)

    def prepare():
        scalars = jnp.concatenate([my_tensor.reshape(1), order ^ my_fsdp]).astype(jnp.int32)

        def kernel(where, student, teacher, x_low, entry, xt_low, to_place, rows_s, rows_t, sems):
            start = pl.multiple_of(where[0] * rows, rows)
            copies = [
                pltpu.make_async_copy(ref.at[pl.ds(start, rows)], to, sems.at[k])
                for k, (ref, to) in enumerate(((student, rows_s), (teacher, rows_t)))
            ]
            for copy in copies:
                copy.start()
            natural = lax.broadcasted_iota(jnp.int32, (width, width), 0)
            place = lax.broadcasted_iota(jnp.int32, (1, width), 1)
            source = place
            for k in range(fsdp):
                inside = (place >= k * depth) & (place < (k + 1) * depth)
                source = jnp.where(inside, place + (where[1 + k] - k) * depth, source)
            to_place[...] = jnp.where(natural == source, 1.0, 0.0).astype(LOW)
            copies[0].wait()
            x = kernel_nn(rows_s[...], to_place[...])
            x_low[...] = x.astype(LOW)
            entry[...] = soft_clip(x).astype(LOW)
            copies[1].wait()
            xt_low[...] = kernel_nn(rows_t[...], to_place[...]).astype(LOW)

        full = ((rows, width), LOW, whole(rows, width))
        have.x_low, have.entry, have.xt_low, have.leave = run.call(
            "place_rows",
            kernel,
            [
                (scalars, SCALARS),
                (student_in, IN_PLACE),
                (teacher_in, IN_PLACE),
            ],
            [full, full, full, ((width, width), LOW, whole(width, width))],
            scratch=[pltpu.VMEM((rows, width), LOW), pltpu.VMEM((rows, width), LOW), pltpu.SemaphoreType.DMA((2,))],
        )

    def prepare_slots():
        units = rows // 64
        first_unit = my_tensor * units

        def kernel(first, sizes, lengths, qid, kid, live_rows):
            for u in range(units):
                unit = first[0] + u
                slot = unit * 64
                size, length = sizes[unit], lengths[unit]
                begin = slot - lax.rem(slot, size)
                here = slice(u * 64, (u + 1) * 64)
                down = slot - begin + lax.broadcasted_iota(jnp.int32, (64, 128), 0)
                kid[here] = jnp.where(down < length, begin, -1)
                live_rows[here] = jnp.where(down < length, 1.0, 0.0)
                across = slot - begin + lax.broadcasted_iota(jnp.int32, (8, 64), 1)
                row = lax.broadcasted_iota(jnp.int32, (8, 64), 0)
                qid[:, here] = jnp.where(row == 0, begin, jnp.where(across < length, 1, 0))

        have.qid, have.kid, have.live_rows = run.call(
            "slots",
            kernel,
            [
                (first_unit.astype(jnp.int32).reshape(1), SCALARS),
                (bucket_size, SCALARS),
                (seq_length, SCALARS),
            ],
            [
                ((8, rows), jnp.int32, whole(8, rows)),
                ((rows, 128), jnp.int32, whole(rows, 128)),
                ((rows, 128), WIDE, whole(rows, 128)),
            ],
        )

    scale = HEAD_DIM ** (-0.5)

    def project_teacher():
        def work(product, refs, here):
            factor = jnp.where(pl.program_id(0) == 0, scale, 1.0)
            return [(product.astype(LOW) * factor.astype(LOW)).astype(LOW)]

        have.proj_t = times_weight(
            run, "project_teacher", have.xt_low, have.w_tqkv, narrow_tiles, work, [], [LOW]
        )[0]

    def project_student():
        def work(product, refs, here):
            factor = jnp.where(pl.program_id(0) == 0, scale, 1.0)
            return [((refs[0][0] * product).astype(LOW) * factor.astype(LOW)).astype(LOW)]

        have.proj_s = times_weight(
            run, "project_student", have.entry, have.w_qkv, narrow_tiles, work,
            [(have.betas, SCALARS)], [LOW],
        )[0]

    def attend(step):
        onto = [have.attended, have.t_attended, have.probs, have.gap] if step else []
        have.attended, have.t_attended, have.probs, have.gap = run_forward(
            run, step, 2, onto, have.qid, have.kid, have.proj_s, have.proj_t
        )

    square = ((rows, width), WIDE)
    square_low = ((rows, width), LOW)

    def close_teacher():
        def work(product, refs, outs, tile):
            here = rows_at(tile)
            normed, _ = norm_parts(refs[0][here].astype(WIDE) + product)
            outs[0][here] = normed
            outs[1][here] = normed.astype(LOW)

        have.t_first, have.t_first_low = times_turned(
            run, "close_teacher", have.t_attended, have.w_tqkv, [3], work,
            [], [have.xt_low], [square, square_low],
        )

    def close_student():
        def work(product, refs, outs, tile):
            betas, gain, x = refs
            here = rows_at(tile)
            normed, size = norm_parts(x[here].astype(WIDE) + betas[1] * product)
            outs[0][here] = normed
            outs[1][here] = jnp.broadcast_to(size, (TILE, 128))
            outs[2][here] = soft_clip(normed * gain[...]).astype(LOW)

        have.n_first, have.r_first, have.middle = times_turned(
            run, "close_student", have.attended, have.w_qkv, [3], work,
            [(have.betas, SCALARS), (have.first_gain, whole(1, width))],
            [have.x_low],
            [square, ((rows, 128), WIDE), square_low],
        )

    def up_teacher():
        def work(product, refs, here):
            return [(product * gelu_cdf(product)).astype(LOW)]

        have.t_hidden = times_weight(
            run, "up_teacher", have.t_first_low, have.w_up, wide_tiles(0), work, [], [LOW]
        )[0]

    def up_student():
        def work(product, refs, here):
            up = refs[0][2] * product
            cdf = gelu_cdf(up)
            return [(up * cdf).astype(LOW), (cdf + up * gelu_density(up)).astype(LOW)]

        have.hidden, have.slope = times_weight(
            run, "up_student", have.middle, have.w_up, wide_tiles(1), work,
            [(have.betas, SCALARS)], [LOW, LOW],
        )

    def down_both():
        parts = have.w_down
        count = len(parts)
        late = [have.t_first, have.n_first, have.live_rows, have.leave]

        def kernel(t_left, s_left, *refs):
            blocks, refs = refs[:count], refs[count:]
            betas, first_gain, second_gain = refs[:3]
            sources = refs[3:7]
            d_second, grad_z, sums, packed = refs[7:11]
            t_total, s_total, weight, t_first, n_first, live_rows, leave, sems = refs[11:]
            j = pl.program_id(0)
            copies = [
                pltpu.make_async_copy(source, to, sems.at[k])
                for k, (source, to) in enumerate(zip(sources, (t_first, n_first, live_rows, leave)))
            ]

            @pl.when(j == 0)
            def _():
                for copy in copies:
                    copy.start()

            row = 0
            for block in blocks:
                weight[pl.ds(row, block.shape[0])] = block[...]
                row += block.shape[0]

            def add(total, left, first):
                product = kernel_nt(left[...], weight[...])

                @pl.when(j == first)
                def _():
                    total[...] = product

                @pl.when(j > first)
                def _():
                    total[...] = total[...] + product

            pl.when(j < tensor)(lambda: add(t_total, t_left, 0))
            pl.when(j >= tensor)(lambda: add(s_total, s_left, tensor))

            @pl.when(j == 2 * tensor - 1)
            def _():
                for copy in copies:
                    copy.wait()
                for tile in range(rows // TILE):
                    here = rows_at(tile)
                    t_result, _ = norm_parts(t_first[here] + t_total[here])
                    normed, size = norm_parts(n_first[here] * first_gain[...] + betas[3] * s_total[here])
                    result = normed * second_gain[...]
                    d_result = jnp.where(live_rows[here][:, 0:1] > 0, result - t_result, 0.0)
                    add_column_sums(sums, d_result * normed, tile)
                    value = norm_back(d_result * second_gain[...], normed, size)
                    d_second[here] = value
                    grad_z[here] = (betas[3] * value).astype(LOW)
                    put_turned(t_result.astype(LOW), leave, packed, tile)
                    put_turned(result.astype(LOW), leave, packed, rows // TILE + tile)

        tiles = pl.BlockSpec((rows, width), lambda j: (0, jnp.clip(j, 0, tensor - 1)))
        later = pl.BlockSpec((rows, width), lambda j: (0, jnp.clip(j - tensor, 0, tensor - 1)))

        def place(j):
            return (0, jnp.where(j < tensor, 2 * j, 2 * (j - tensor) + 1))

        have.d_second, have.grad_z, have.sums_second, have.leaving = run.call(
            "down_both",
            kernel,
            [(have.t_hidden, tiles), (have.hidden, later)]
            + [(part, pl.BlockSpec((part.shape[0], width), place)) for part in parts]
            + [
                (have.betas, SCALARS),
                (have.first_gain, whole(1, width)),
                (have.second_gain, whole(1, width)),
            ]
            + [(value, IN_PLACE) for value in late],
            [
                (shape, dtype, whole(*shape))
                for shape, dtype in (square, square_low, ((8, width), WIDE), ((width, 2 * rows), LOW))
            ],
            grid=(2 * tensor,),
            scratch=[pltpu.VMEM((rows, width), WIDE), pltpu.VMEM((rows, width), WIDE), pltpu.VMEM((width, width), LOW)]
            + [pltpu.VMEM(value.shape, value.dtype) for value in late]
            + [pltpu.SemaphoreType.DMA((4,))],
            flops=4 * rows * width * hidden_width,
            moved=4 * (rows * hidden_width + width * hidden_width),
        )


    def split_one(a, b):
        return tuple(value.reshape(depth, tensor // 2, -1).transpose(1, 0, 2) for value in (a, b))

    def split_qkv(a, b):
        value = jnp.concatenate([a, b], axis=1).reshape(depth, 3, tensor, part).transpose(2, 0, 1, 3)
        value = value.reshape(tensor, depth, 3 * part)
        return value[: tensor // 2], value[tensor // 2 :]

    def share_down():
        return Task(scatter_weight(run, "g_down", have.grad_z, have.hidden, None, keep("grad_down")))

    def back_down():
        def work(product, refs, here):
            return [(refs[0][2] * (product * refs[1][here].astype(WIDE))).astype(LOW)]

        have.grad_u = times_weight(
            run, "back_down", have.grad_z, have.w_down, wide_tiles(1), work,
            [(have.betas, SCALARS), (have.slope, pl.BlockSpec((rows, width), lambda j: (0, j)))],
            [LOW],
        )[0]

    def share_up():
        return Task(scatter_weight(run, "g_up", have.middle, have.grad_u, None, keep("grad_up")))

    def back_up():
        def work(product, refs, outs, tile):
            betas, gain, d_second, n_first, r_first, w_out = refs
            here = rows_at(tile)
            normed = n_first[here]
            d_h = d_second[here] + product * clip_slope(normed * gain[...])
            add_column_sums(outs[3], d_h * normed, tile)
            d_first = norm_back(d_h * gain[...], normed, r_first[here][:, 0:1])
            outs[0][here] = d_first
            grad_o = (betas[1] * d_first).astype(LOW)
            outs[1][here] = grad_o
            outs[2][here] = kernel_nn(grad_o, w_out[...]).astype(LOW)

        have.d_first, have.grad_o, have.d_attended, have.sums_first = times_turned(
            run, "back_up", have.grad_u, have.w_up, wide_tiles(1), work,
            [(have.betas, SCALARS), (have.first_gain, whole(1, width))],
            [have.d_second, have.n_first, have.r_first, (have.w_qkv, 3 * width)],
            [square, square_low, square_low, ((8, width), WIDE)],
        )

    def share_out():
        beside = (have.sums_first, have.sums_second)
        return Task(
            scatter_weight(run, "g_out", have.grad_o, have.attended, split_one, keep("grad_out"), beside)
        )

    def back_attend():
        have.g_all = run_backward(
            run, have.betas, have.proj_s, have.d_attended, have.probs, have.gap
        )

    def share_qkv():
        return Task(scatter_weight(run, "g_qkv", have.entry, have.g_all, split_qkv, keep("grad_qkv"), triple=True))

    def back_entry():
        def work(product, refs, outs, tile):
            here = rows_at(tile)
            x = refs[1][here].astype(WIDE)
            put_turned((refs[0][here] + product * clip_slope(x)).astype(LOW), refs[2], outs[0], tile)

        have.g_leave = times_turned(
            run, "back_entry", have.g_all, have.w_qkv, narrow_tiles, work,
            [], [have.d_first, have.x_low, have.leave], [packed],
        )[0]

    def bring(name, shard, finish_rows):
        return Task(gather_weight(run, name, shard, finish_rows, keep(name)))

    ta = bring("w_tqkv", shard_tqkv, finish_qkv)
    sa = bring("w_qkv", shard_qkv, finish_qkv)
    c = bring("w_up", shard_up, None)
    d = bring("w_down", shard_down, None)
    go_on(ta)
    run.wait(run.shards[0])
    small = Task(gather_small(gains, magnitudes(), small_store))
    go_on(sa)
    go_on(small)
    run.land(small)
    prepare_slots()
    go_on(small)
    run.land(small)
    go_on(ta)
    go_on(small)
    prepare()
    run.land(small)
    go_on(sa)
    go_on(ta)
    run.land(ta, only=0)
    run.fence()
    go_on(ta)
    run.land(sa)
    go_on(c)
    run.land(ta)
    go_on(sa)
    go_on(d)
    go_on(small)
    go_on(ta)
    run.land(ta, only=1)
    run.land(sa, only=0)
    run.fence()
    go_on(ta)
    go_on(sa)
    run.land(sa)
    run.land(small)
    run.fence()
    go_on(small)
    go_on(sa)
    run.land(sa, only=1)
    run.land(small)
    run.fence()
    finish(small)
    go_on(sa)
    finish(ta)
    go_on(c)
    go_on(c)
    project_teacher()
    finish(sa)
    project_student()
    attend(0)
    run.land(c, d)
    run.fence()
    go_on(c)
    go_on(c)
    attend(1)
    go_on(d)
    go_on(d)
    close_teacher()
    run.land(c)
    close_student()
    finish(c)
    run.land(d, only=0)
    up_teacher()
    run.land(d, only=1)
    run.fence()
    go_on(d)
    go_on(d)
    up_student()
    run.land(d)
    run.fence()
    finish(d)
    down_both()
    leaving = Task(leave_columns(run, "arrive", have.leaving, LOW, 2, keep("teacher_out", "student_out")))
    go_on(leaving)
    down = share_down()
    go_on(down)
    back_down()
    up = share_up()
    go_on(up)
    go_on(down)
    go_on(up)
    back_up()
    go_on(down)
    back_attend()
    go_on(down)
    go_on(up)
    qkv = share_qkv()
    go_on(qkv)
    run.land(down, leaving)
    go_on(up)
    go_on(down)
    back_entry()
    g_leave = Task(leave_columns(run, "arrive_grad", have.g_leave, WIDE, 1, keep("input_grad")))
    go_on(g_leave)
    run.land(down, up)
    go_on(qkv)
    go_on(up)
    out = share_out()
    go_on(out)
    go_on(out)
    go_on(qkv)
    finish(leaving)
    go_on(qkv)
    go_on(out)
    finish(g_leave)
    go_on(out)
    finish(qkv)
    finish(out)
    finish(up)
    finish(down)

    def inside(grad, latent):
        return jnp.where(jnp.abs(latent) <= 1.0, grad, 0.0)

    return (
        have.student_out,
        have.teacher_out,
        have.input_grad,
        inside(have.grad_qkv.reshape(depth, 3, part).transpose(1, 0, 2), qkv_latent),
        inside(have.grad_out[:, :part].T, out_latent),
        inside(have.grad_up, up_latent),
        inside(have.grad_down.T, down_latent),
        have.grad_out[:, part],
        have.grad_out[:, part + 1],
    )


def solution(mesh):
    placed = (
        P(FSDP, None),
        P(FSDP, None),
        P(FSDP),
        P(FSDP),
        P(None, FSDP, TENSOR),
        P(TENSOR, FSDP),
        P(FSDP, TENSOR),
        P(TENSOR, FSDP),
        P(FSDP),
        P(FSDP),
        P(None, FSDP, TENSOR),
        P(TENSOR, FSDP),
        P(FSDP, TENSOR),
        P(TENSOR, FSDP),
    )
    return jax.shard_map(
        body,
        mesh=mesh,
        in_specs=placed,
        out_specs=(
            P(FSDP, TENSOR),
            P(FSDP, TENSOR),
            P(FSDP, TENSOR),
            P(None, FSDP, TENSOR),
            P(TENSOR, FSDP),
            P(FSDP, TENSOR),
            P(TENSOR, FSDP),
            P(FSDP),
            P(FSDP),
        ),
        check_vma=False,
    )
```

```python
import functools
import math
import types

import jax
import jax.numpy as jnp
from jax import lax
from jax.experimental import pallas as pl
from jax.experimental.pallas import tpu as pltpu
from jax.sharding import PartitionSpec as P

HEAD_DIM = 64
PAIR = 2 * HEAD_DIM
TILE = 256
CLIP_RANGE = 2.5
ATT_WEIGHT = 0.015625
EPSILON = 1e-06
NEG_FILL = -1000000000.0
LOW = jnp.bfloat16
WIDE = jnp.float32
FSDP = "fsdp"
TENSOR = "tensor"
VMEM_BYTES = 60 * 1024 * 1024
WEIGH = 5


IN_PLACE = pl.BlockSpec(memory_space=pl.ANY)
SCALARS = pl.BlockSpec(memory_space=pltpu.SMEM)


class Task:
    def __init__(self, stages):
        self.stages = stages
        self.arrays = None

    def go_on(self):
        try:
            got = next(self.stages) if self.arrays is None else self.stages.send(self.arrays)
            self.arrays = list(got)
        except StopIteration:
            self.arrays = ()

    def finish(self):
        while self.arrays != ():
            self.go_on()


class Order:
    def __init__(self):
        self.after = []
        self.landing = []
        self.shards = []

    def land(self, *tasks, only=None):
        for task in tasks:
            for k in range(len(task.arrays)):
                if only is None or only == k:
                    self.landing.append((task, k))

    def wait(self, *arrays):
        self.after = self.after + list(arrays)

    def fence(self):
        def kernel(out):
            out[...] = jnp.zeros((8, 128), WIDE)

        self.call("fence", kernel, [], [((8, 128), WIDE, whole(8, 128))])

    def call(self, name, kernel, ins, outs, grid=(1,), scratch=(), flops=0, moved=0, onto=()):
        waits = [value for value in self.after if not any(value is array for array in onto)]
        passed = [task.arrays[k] for task, k in self.landing]
        count, given = len(ins), len(outs)
        skip = len(onto) + len(passed) + len(waits)

        def wrapped(*refs):
            kernel(*refs[:count], *refs[count + skip : count + skip + given], *refs[count + skip + given + len(passed) :])

        aliases = {count + k: k for k in range(len(onto))}
        aliases.update({count + len(onto) + k: given + k for k in range(len(passed))})
        results = pl.pallas_call(
            wrapped,
            grid=grid,
            in_specs=[spec for _, spec in ins] + [IN_PLACE] * skip,
            out_specs=[spec for _, _, spec in outs] + [IN_PLACE] * len(passed),
            out_shape=[jax.ShapeDtypeStruct(shape, dtype) for shape, dtype, _ in outs]
            + [jax.ShapeDtypeStruct(array.shape, array.dtype) for array in passed],
            scratch_shapes=list(scratch),
            input_output_aliases=aliases,
            compiler_params=pltpu.CompilerParams(vmem_limit_bytes=VMEM_BYTES),
            cost_estimate=pl.CostEstimate(flops=flops * WEIGH, bytes_accessed=moved * WEIGH, transcendentals=0),
            name=name,
        )(*[array for array, _ in ins], *onto, *passed, *waits)
        rest = list(results[given:])
        for task, k in self.landing:
            task.arrays[k] = rest.pop(0)
        self.landing = []
        self.after = [results[0]]
        return list(results[:given])


def whole(*shape):
    return pl.BlockSpec(shape, lambda *_: (0,) * len(shape))


def swap(value, axis, bit):
    size = lax.axis_size(axis)
    return lax.ppermute(value, axis, [(i, i ^ bit) for i in range(size)])


def swap_first(value):
    return lax.ppermute(value, FSDP, [(i, i ^ (4 if i % 2 else 2)) for i in range(8)])


def swap_second(value):
    return lax.ppermute(value, FSDP, [(i, i ^ (2 if i % 2 else 4)) for i in range(8)])


def bits_of(axis):
    size = lax.axis_size(axis)
    bits = [1 << k for k in range(size.bit_length() - 1)]
    return [bits[0]] + bits[:0:-1] if bits else []


def order_of(axis):
    order = [0]
    for bit in reversed(bits_of(axis)):
        order = order + [o ^ bit for o in order]
    return order


def two_links(rows):
    return lax.axis_size(FSDP) == 8 and rows % 32 == 0


CHIP_ORDERS = ([0, 2, 4, 6, 1, 5, 3, 7], [0, 4, 2, 6, 1, 3, 5, 7])


def feature_order(depth):
    if not two_links(depth):
        return jnp.array(order_of(FSDP), jnp.int32)
    odd = lax.axis_index(FSDP) & 1
    return jnp.where(odd > 0, jnp.array(CHIP_ORDERS[1], jnp.int32), jnp.array(CHIP_ORDERS[0], jnp.int32))


def reorder(blocks, back):
    plain = order_of(FSDP)
    results = []
    for chip in CHIP_ORDERS:
        if back:
            results.append([blocks[chip.index(m)] for m in plain])
        else:
            results.append([blocks[plain.index(m)] for m in chip])
    odd = lax.axis_index(FSDP) & 1
    return [jnp.where(odd > 0, two, one) for one, two in zip(*results)]


def join_columns(run, name, arrays, moves, columns):
    rows = arrays[0].shape[0]

    def kernel(*refs):
        for k, source, target, count in moves:
            refs[-1][:, target : target + count] = refs[k][:, source : source + count]

    return run.call(
        name,
        kernel,
        [(array, whole(*array.shape)) for array in arrays],
        [((rows, columns), LOW, whole(rows, columns))],
        moved=4 * rows * columns,
    )[0]


def side_by_side(run, name, left, right):
    n = left.shape[1]
    return join_columns(run, name, [left, right], [(0, 0, 0, n), (1, 0, n, n)], 2 * n)


def rows_in_order(run, name, near, far):
    rows, wide = near.shape
    n = wide // 2
    places = lax.axis_index(TENSOR) ^ jnp.array([0, 2, 1, 3], jnp.int32)

    def kernel(where, near_ref, far_ref, out):
        for k in range(4):
            ref = near_ref if k < 2 else far_ref
            start = pl.multiple_of(where[k] * n, 128)
            out[:, pl.ds(start, n)] = ref[:, (k % 2) * n : (k % 2 + 1) * n]

    return run.call(
        name,
        kernel,
        [(places, SCALARS), (near, whole(rows, wide)), (far, whole(rows, wide))],
        [((rows, 2 * wide), LOW, whole(rows, 2 * wide))],
    )[0]


def gather_weight(run, name, shard, finish, store):
    value = shard()
    run.shards.append(value)
    if finish is None:
        (got,) = yield [swap(value, TENSOR, 2)]
        value = side_by_side(run, name + "_join", value, got)
        (got,) = yield [swap(value, TENSOR, 1)]
        mine = rows_in_order(run, name + "_rows", value, got)
    else:
        (got,) = yield [swap(value, TENSOR, 2)]
        value = side_by_side(run, name + "_join", value, got)
        (got,) = yield [swap(value, TENSOR, 1)]
        mine = finish(name + "_rows", value, got)
    if two_links(mine.shape[0]):
        sibling, first = yield [swap(mine, FSDP, 1), swap_first(mine)]
        first, first_other = yield [first, swap_first(sibling)]
        second_other, second = yield [swap(first, FSDP, 1), swap(first_other, FSDP, 1)]
        (both,) = yield [swap_first(second)]
        both_other = swap(both, FSDP, 1)
        store((mine, first, second, both, sibling, second_other, first_other, both_other))
    else:
        for bit in reversed(bits_of(FSDP)):
            mine = jnp.concatenate([mine, swap(mine, FSDP, bit)], axis=0)
        store((mine,))


def add_low(left, right):
    return (left.astype(WIDE) + right.astype(WIDE)).astype(LOW)


def scatter_weight(run, name, left, right, split, store, beside=None, triple=False):
    rows, width = left.shape
    fsdp = lax.axis_size(FSDP)
    depth = width // fsdp
    columns = right.shape[1]
    middle, half = width // 2, columns // 2
    step = half
    steps = half // step
    side = pl.BlockSpec((rows, step), lambda j: (0, j))
    cost = dict(flops=2 * rows * middle * columns, moved=2 * (rows * columns + 2 * middle * columns))
    added = []
    out_step = step
    if beside is not None:
        added = [(value, whole(8, width)) for value in beside]
        lanes = step // 2
        out_step = 2 * (lanes + 64)
        half = steps * out_step
        columns = 2 * half

    def product(left_ref, right_ref, sums, start):
        value = kernel_tn(left_ref[...], right_ref[...])
        if not sums:
            return value
        turned = [
            jnp.broadcast_to(jnp.sum(ref[:, start : start + middle], axis=0, keepdims=True), (128, middle)).T for ref in sums
        ]
        lane = lax.broadcasted_iota(jnp.int32, (middle, 128), 1)
        more = jnp.where(lane == 0, turned[0], jnp.where(lane == 1, turned[1], 0.0))[:, :64]
        return jnp.concatenate([value[:, :lanes], more, value[:, lanes:], more], axis=1)

    def far_kernel(left_ref, right_ref, *refs):
        refs[-1][...] = product(left_ref, right_ref, refs[:-1], middle).astype(LOW)

    far = run.call(
        name + "_far",
        far_kernel,
        [(left, pl.BlockSpec((rows, middle), lambda j: (0, 1))), (right, side)] + added,
        [((middle, columns), LOW, pl.BlockSpec((middle, out_step), lambda j: (0, j)))],
        grid=(2 * steps,),
        **cost,
    )[0]
    (got,) = yield [swap(far, FSDP, 1)]
    near_ins = [
        (left, pl.BlockSpec((rows, middle), lambda j: (0, 0))),
        (right, side),
        (got, pl.BlockSpec((middle, out_step), lambda j: (0, j))),
    ] + added
    if two_links(depth):
        one = ((depth, columns), LOW, whole(depth, columns))
        at = [slice(k * depth, (k + 1) * depth) for k in range(4)]

        def near_kernel(left_ref, right_ref, got_ref, *refs):
            keep, send = refs[-2:]
            total = (product(left_ref, right_ref, refs[:-2], 0) + got_ref[...].astype(WIDE)).astype(LOW)
            keep[at[0]], keep[at[1]] = total[at[0]], total[at[2]]
            send[at[0]], send[at[1]] = total[at[1]], total[at[3]]

        def second(keep, got, own, onward):
            own[...] = add_low(keep[at[0]], got[at[0]])
            onward[...] = add_low(keep[at[1]], got[at[1]])

        def third(own, got, *outs):
            n = columns // len(outs)
            for k, out in enumerate(outs):
                lanes = slice(k * n, (k + 1) * n)
                out[...] = add_low(own[:, lanes], got[:, lanes])

        def third_split(own, got, keep, send):
            n = columns // 12
            for p in range(4):
                out = keep if p < 2 else send
                for k in range(3):
                    lanes = slice((4 * k + p) * n, (4 * k + p + 1) * n)
                    out[at[p % 2], k * n : (k + 1) * n] = add_low(own[:, lanes], got[:, lanes])

        def third_rows(where, own, got, keep, send):
            n = columns // 4
            for k in range(4):
                lanes = slice(k * n, (k + 1) * n)
                row = pl.multiple_of((where[k] & 1) * depth, depth)

                @pl.when(where[k] < 2)
                def _():
                    keep[pl.ds(row, depth)] = add_low(own[:, lanes], got[:, lanes])

                @pl.when(where[k] >= 2)
                def _():
                    send[pl.ds(row, depth)] = add_low(own[:, lanes], got[:, lanes])

        pair = ((2 * depth, columns), LOW, pl.BlockSpec((2 * depth, out_step), lambda j: (0, j)))
        keep, send = run.call(name + "_near", near_kernel, near_ins, [pair] * 2, grid=(2 * steps,), **cost)
        (got,) = yield [swap_first(send)]
        full = whole(2 * depth, columns)
        own, onward = run.call(name + "_add2", second, [(keep, full), (got, full)], [one] * 2, moved=6 * depth * columns)
        (got,) = yield [swap_second(onward)]
        ins = [(own, one[2]), (got, one[2])]
        if split is None:
            shape = (2 * depth, columns // 4)
            m = jnp.arange(4, dtype=jnp.int32) ^ lax.axis_index(TENSOR)
            ins = [((m & 1) * 2 + (m >> 1), SCALARS)] + ins
            here = run.call(
                name + "_add3", third_rows, ins, [(shape, LOW, whole(*shape))] * 2, moved=6 * depth * columns
            )
            split = lambda *parts: tuple(value.reshape(2, depth, -1) for value in parts)
        else:
            shape = (2 * depth, columns // 4) if triple else (depth, half)
            work = third_split if triple else third
            here = run.call(name + "_add3", work, ins, [(shape, LOW, whole(*shape))] * 2, moved=6 * depth * columns)
            if triple:
                split = lambda *parts: tuple(value.reshape(2, depth, -1) for value in parts)
    else:

        def near_kernel(left_ref, right_ref, got_ref, *refs):
            value = product(left_ref, right_ref, refs[:-1], 0)
            refs[-1][...] = (value + got_ref[...].astype(WIDE)).astype(LOW)

        here = run.call(
            name + "_near",
            near_kernel,
            near_ins,
            [((middle, columns), LOW, pl.BlockSpec((middle, out_step), lambda j: (0, j)))],
            grid=(2 * steps,),
            **cost,
        )[0].reshape(fsdp // 2, depth, columns)
        count = fsdp // 2
        for bit in bits_of(FSDP)[1:]:
            count //= 2
            (got,) = yield [swap(here[count:], FSDP, bit)]
            here = add_low(here[:count], got)
        if split is None:
            here = here[0].reshape(depth, 4, -1).transpose(1, 0, 2).reshape(4 * depth, -1)
        else:
            here = (here[0, :, :half], here[0, :, half:])
    if split is None:
        (here,) = yield [lax.psum_scatter(here, TENSOR, scatter_dimension=0, tiled=True)]
        store(here.astype(WIDE))
        return
    keep, send = split(*here)
    for bit in bits_of(TENSOR):
        (got,) = yield [swap(send, TENSOR, bit)]
        total = add_low(keep, got)
        keep, send = total[: total.shape[0] // 2], total[total.shape[0] // 2 :]
    store(total[0].astype(WIDE))


def gather_small(gains, sums, store):
    depth = gains.shape[1]
    block = jnp.concatenate([sums, jnp.pad(gains, ((0, 6), (0, 128 - depth)))], axis=0)[None]
    for bit in reversed(bits_of(FSDP)):
        (got,) = yield [swap(block, FSDP, bit)]
        block = jnp.concatenate([block, got], axis=0)
    parts = [block[k, 8:10, :depth] for k in range(block.shape[0])]
    gains = jnp.concatenate(reorder(parts, False) if two_links(depth) else parts, axis=1)
    sums = block[:, :8]
    while sums.shape[0] > 1:
        sums = sums[: sums.shape[0] // 2] + sums[sums.shape[0] // 2 :]
    sums = sums[0]
    for bit in bits_of(TENSOR):
        (got,) = yield [swap(sums, TENSOR, bit)]
        sums = sums + got
    store(gains, sums[0])


def leave_columns(run, name, value, dtype, count, store):
    size = lax.axis_size(TENSOR)
    (got,) = yield [lax.all_to_all(value, TENSOR, 0, 0, tiled=True)]
    columns, rows = got.shape[0] // size, got.shape[1] // count

    def kernel(ref, *outs):
        for k, out in enumerate(outs):
            out[...] = ref[:, k * rows : (k + 1) * rows].astype(dtype)

    results = run.call(
        name,
        kernel,
        [(got, pl.BlockSpec((columns, count * rows), lambda i: (i, 0)))],
        [((columns, size * rows), dtype, pl.BlockSpec((columns, rows), lambda i: (0, i)))] * count,
        grid=(size,),
        moved=8 * columns * rows,
    )
    store(*[result.T for result in results])


def put_turned(value, natural, out, tile):
    out[:, tile * TILE : (tile + 1) * TILE] = kernel_nt(natural[...], value).astype(LOW)


def dot(left, right):
    return jnp.dot(left, right, preferred_element_type=WIDE)


def dot_tn(left, right):
    return lax.dot_general(left, right, (((0,), (0,)), ((), ())), preferred_element_type=WIDE)


def dot_nt(left, right):
    return lax.dot_general(left, right, (((1,), (1,)), ((), ())), preferred_element_type=WIDE)


def soft_clip(value):
    return CLIP_RANGE * jnp.tanh(value / CLIP_RANGE)


def clip_slope(value):
    bent = jnp.tanh(value / CLIP_RANGE)
    return 1.0 - bent * bent


def norm_parts(value):
    centre = value - jnp.mean(value, axis=-1, keepdims=True)
    scale = lax.rsqrt(jnp.mean(centre * centre, axis=-1, keepdims=True) + EPSILON)
    return centre * scale, scale


def norm_back(grad, normed, scale):
    return scale * (
        grad
        - jnp.mean(grad, axis=-1, keepdims=True)
        - normed * jnp.mean(grad * normed, axis=-1, keepdims=True)
    )


def gelu_cdf(value):
    return 0.5 + 0.5 * lax.erf(value * math.sqrt(0.5))


def gelu_density(value):
    return jnp.exp(-0.5 * value * value) * (1.0 / math.sqrt(2.0 * math.pi))


def kernel_nt(left, right):
    return lax.dot_general(left, right, (((1,), (1,)), ((), ())), preferred_element_type=WIDE)


def kernel_tn(left, right):
    return lax.dot_general(left, right, (((0,), (0,)), ((), ())), preferred_element_type=WIDE)


def kernel_nn(left, right):
    return jnp.dot(left, right, preferred_element_type=WIDE)


def times_weight(run, name, left, parts, tiles, work, extras, outs):
    rows, width = left.shape
    base, stride = tiles[0], tiles[1] - tiles[0]
    count = len(parts)

    def kernel(*refs):
        weight = refs[-1]
        row = 0
        for block in refs[1 : 1 + count]:
            weight[pl.ds(row, block.shape[0])] = block[...]
            row += block.shape[0]
        for r in range(0, rows, TILE):
            here = pl.ds(r, TILE)
            values = work(kernel_nn(refs[0][here], weight[...]), refs[1 + count : 1 + count + len(extras)], here)
            for ref, value in zip(refs[1 + count + len(extras) : -1], values):
                ref[here] = value

    columns = width * len(tiles)
    return run.call(
        name,
        kernel,
        [(left, whole(rows, width))]
        + [(part, pl.BlockSpec((part.shape[0], width), lambda j: (0, base + stride * j))) for part in parts]
        + extras,
        [((rows, columns), dtype, pl.BlockSpec((rows, width), lambda j: (0, j))) for dtype in outs],
        grid=(len(tiles),),
        scratch=[pltpu.VMEM((width, width), LOW)],
        flops=2 * rows * width * columns,
        moved=2 * (rows * width + width * columns + len(outs) * rows * columns),
    )


def times_turned(run, name, left, parts, tiles, work, extras, late, outs):
    rows, wide = left.shape
    width = sum(part.shape[0] for part in parts)
    step = wide // len(tiles)
    base, stride = tiles[0], tiles[1] - tiles[0] if len(tiles) > 1 else 1
    count, more = len(parts), len(extras)
    sources, held = [], []
    for item in late:
        pieces, column = item if isinstance(item, tuple) else ([item], 0)
        columns = pieces[0].shape[1] if column == 0 and not isinstance(item, tuple) else width
        row = 0
        for piece in pieces:
            sources.append((piece, len(held), row, column, columns))
            row += piece.shape[0]
        held.append(pltpu.VMEM((row, columns), pieces[0].dtype))
    first_late = 1 + count + more
    first_out = first_late + len(sources)
    first_held = first_out + len(outs) + 2

    def kernel(*refs):
        total, weight = refs[first_out + len(outs)], refs[first_out + len(outs) + 1]
        scratch, sems = refs[first_held:-1], refs[-1]
        j = pl.program_id(0)
        copies = []
        for k, (piece, to, row, column, columns) in enumerate(sources):
            copies.append(
                pltpu.make_async_copy(
                    refs[first_late + k].at[:, pl.ds(column, columns)],
                    scratch[to].at[pl.ds(row, piece.shape[0])],
                    sems.at[k],
                )
            )

        @pl.when(j == 0)
        def _():
            for copy in copies:
                copy.start()

        row = 0
        for block in refs[1 : 1 + count]:
            weight[pl.ds(row, block.shape[0])] = block[...]
            row += block.shape[0]
        product = kernel_nt(refs[0][...], weight[...])

        @pl.when(j == 0)
        def _():
            total[...] = product

        @pl.when(j > 0)
        def _():
            total[...] = total[...] + product

        @pl.when(j == len(tiles) - 1)
        def _():
            for copy in copies:
                copy.wait()
            for tile in range(rows // TILE):
                work(
                    total[pl.ds(tile * TILE, TILE)],
                    list(refs[1 + count : first_late]) + list(scratch),
                    refs[first_out : first_out + len(outs)],
                    tile,
                )

    return run.call(
        name,
        kernel,
        [(left, pl.BlockSpec((rows, step), lambda j: (0, j)))]
        + [(part, pl.BlockSpec((part.shape[0], step), lambda j: (0, base + stride * j))) for part in parts]
        + extras
        + [(piece, IN_PLACE) for piece, _, _, _, _ in sources],
        [(shape, dtype, whole(*shape)) for shape, dtype in outs],
        grid=(len(tiles),),
        scratch=[pltpu.VMEM((rows, width), WIDE), pltpu.VMEM((width, step), LOW)]
        + held
        + [pltpu.SemaphoreType.DMA((max(len(sources), 1),))],
        flops=2 * rows * width * wide,
        moved=2 * (rows * wide + width * wide),
    )


def rows_at(tile):
    return pl.ds(tile * TILE, TILE)


def tile_rows(columns):
    return pl.BlockSpec((TILE, columns), lambda i: (i, 0))


def add_column_sums(ref, value, tile):
    total = jnp.sum(value.reshape(value.shape[0] // 8, 8, value.shape[1]), axis=0)
    ref[...] = total if tile == 0 else ref[...] + total


def both_heads(value):
    first = lax.broadcasted_iota(jnp.int32, (1, PAIR), 1) < HEAD_DIM
    zero = jnp.zeros((), value.dtype)
    return jnp.concatenate([jnp.where(first, value, zero), jnp.where(first, zero, value)], axis=0)


def own_heads(value):
    return jnp.concatenate([value[:HEAD_DIM, :TILE], value[HEAD_DIM:, TILE:]], axis=0).T


def attend_forward(qid, kid, qs, ks, vs, qt, kt, vt, os, ot, probs_out, gap_out):
    keep = kid[:, 0:1] == qid[0:1, :]
    both = keep & (qid[1:2, :] > 0)
    bias = jnp.where(keep, 0.0, NEG_FILL)
    bias = jnp.concatenate([bias, bias], axis=1)
    seen = jnp.where(both, 1.0, 0.0)
    seen = jnp.concatenate([seen, seen], axis=1)

    def soft(score):
        masked = score + bias
        expo = jnp.exp(masked - jnp.max(masked, axis=0, keepdims=True))
        return (expo * (1.0 / jnp.sum(expo, axis=0, keepdims=True))).astype(LOW)

    for p in range(qs.shape[1] // PAIR):
        here = slice(p * PAIR, (p + 1) * PAIR)
        score_s = kernel_nt(ks[:, here], both_heads(qs[:, here]))
        score_t = kernel_nt(kt[:, here], both_heads(qt[:, here]))
        gap_out[0, p] = ((score_s - score_t) * seen).astype(LOW)
        probs = soft(score_s)
        probs_out[0, p] = probs
        os[:, here] = own_heads(kernel_tn(vs[:, here], probs)).astype(LOW)
        ot[:, here] = own_heads(kernel_tn(vt[:, here], soft(score_t))).astype(LOW)


def attend_backward(betas, proj, grad, probs, gap, out):
    width = grad.shape[1]
    up = jnp.asarray(1.0 / ATT_WEIGHT, LOW)
    b = betas[0] * ATT_WEIGHT
    scale = HEAD_DIM ** (-0.5)
    for p in range(width // PAIR):
        at_q = slice(p * PAIR, (p + 1) * PAIR)
        at_k = slice(width + p * PAIR, width + (p + 1) * PAIR)
        at_v = slice(2 * width + p * PAIR, 2 * width + (p + 1) * PAIR)
        grad_two = both_heads(grad[:, at_q] * up)
        prob_low = probs[0, p]
        prob = prob_low.astype(WIDE)
        weighted = prob * kernel_nt(proj[:, at_v], grad_two)
        inner = jnp.sum(weighted, axis=0, keepdims=True)
        d_score = (weighted - prob * inner + gap[0, p].astype(WIDE)).astype(LOW)
        out[:, at_v] = (b * kernel_nn(prob_low, grad_two)).astype(LOW)
        out[:, at_k] = (b * kernel_nn(d_score, both_heads(proj[:, at_q]))).astype(LOW)
        out[:, at_q] = own_heads((b * scale) * kernel_tn(proj[:, at_k], d_score)).astype(LOW)


def run_forward(run, step, steps, onto, qid, kid, proj_s, proj_t):
    rows, wide = proj_s.shape
    width = wide // 3
    pairs = width // PAIR
    tiles = rows // TILE

    def part(j):
        return pl.BlockSpec((TILE, width // steps), lambda b: (b, j * steps + step))

    square = pl.BlockSpec((1, pairs // steps, TILE, 2 * TILE), lambda b: (b, step, 0, 0))
    return run.call(
        "attend_forward",
        attend_forward,
        [(qid, pl.BlockSpec((8, TILE), lambda b: (0, b))), (kid, pl.BlockSpec((TILE, 128), lambda b: (b, 0)))]
        + [(value, part(j)) for value in (proj_s, proj_t) for j in range(3)],
        [((rows, width), LOW, part(0))] * 2 + [((tiles, pairs, TILE, 2 * TILE), LOW, square)] * 2,
        grid=(tiles,),
        flops=32 * rows * TILE * width // steps,
        moved=8 * rows * wide // steps,
        onto=onto,
    )


def run_backward(run, betas, proj_s, grad, probs, gap):
    rows, wide = proj_s.shape
    width = wide // 3
    pairs = width // PAIR
    square = pl.BlockSpec((1, pairs, TILE, 2 * TILE), lambda b: (b, 0, 0, 0))
    return run.call(
        "attend_backward",
        attend_backward,
        [(betas, SCALARS), (proj_s, tile_rows(wide)), (grad, tile_rows(width)), (probs, square), (gap, square)],
        [((rows, wide), LOW, tile_rows(wide))],
        grid=(rows // TILE,),
        flops=16 * rows * TILE * width,
        moved=8 * rows * wide,
    )[0]


def body(
    student_in,
    teacher_in,
    bucket_size,
    seq_length,
    qkv_latent,
    out_latent,
    up_latent,
    down_latent,
    gain_attn,
    gain_ffn,
    teach_qkv,
    teach_out,
    teach_up,
    teach_down,
):
    width = student_in.shape[1]
    fsdp = lax.axis_size(FSDP)
    tensor = lax.axis_size(TENSOR)
    rows = student_in.shape[0] // tensor
    depth = width // fsdp
    hidden_width = up_latent.shape[1] * tensor
    my_fsdp = lax.axis_index(FSDP)
    my_tensor = lax.axis_index(TENSOR)
    first_row = my_tensor * rows
    order = feature_order(depth)
    order_t = order_of(TENSOR)

    have = types.SimpleNamespace()
    run = Order()

    def keep(*names):
        def store(*values):
            for name, value in zip(names, values):
                setattr(have, name, value)

        return store

    def go_on(*tasks):
        for task in tasks:
            task.go_on()

    def finish(*tasks):
        for task in tasks:
            task.finish()

    gains = jnp.stack([gain_attn, gain_ffn]).astype(WIDE)

    def magnitudes():
        latents = (qkv_latent.reshape(-1, qkv_latent.shape[2]), out_latent, up_latent, down_latent)

        def kernel(*refs):
            lane = lax.broadcasted_iota(jnp.int32, (8, 128), 1)
            total = jnp.zeros((8, 128), WIDE)
            for k in range(4):
                total = jnp.where(lane == k, jnp.sum(jnp.abs(refs[k][...])), total)
            refs[4][...] = total

        return run.call(
            "magnitudes", kernel, [(value, whole(*value.shape)) for value in latents], [((8, 128), WIDE, whole(8, 128))]
        )[0]

    def pack_qkv(value):
        return value.astype(LOW).transpose(1, 0, 2).reshape(depth, -1)

    part = width // tensor

    def finish_qkv(name, near, far):
        moves = []
        for p in range(tensor):
            for k in range(4):
                moves.append((p // 2, (p % 2) * 4 * part + k * part, k * width + p * part, part))
        return join_columns(run, name, [near, far], moves, 4 * width)

    narrow_tiles = [0, 1, 2]

    def wide_tiles(which):
        return [2 * p + which for p in range(tensor)]

    def signs(value):
        return jnp.sign(value).astype(LOW)


    def shard_tqkv():
        return jnp.concatenate([pack_qkv(teach_qkv), teach_out.T], axis=1)

    def shard_qkv():
        return jnp.concatenate([pack_qkv(signs(qkv_latent)), signs(out_latent).T], axis=1)

    def pack_signs(name, teach, latent):
        def kernel(teach_ref, latent_ref, out):
            value = latent_ref[...]
            n = value.shape[1]
            out[:, :n] = teach_ref[...]
            out[:, n:] = jnp.where(value > 0, 1.0, jnp.where(value < 0, -1.0, 0.0)).astype(LOW)

        r, n = teach.shape
        return run.call(
            name, kernel, [(teach, whole(r, n)), (latent, whole(r, n))], [((r, 2 * n), LOW, whole(r, 2 * n))]
        )[0]

    def shard_up():
        return pack_signs("pack_up", teach_up, up_latent)

    def shard_down():
        return pack_signs("pack_down", teach_down.T, down_latent.T)

    def small_store(all_gains, totals):
        have.first_gain = all_gains[0:1]
        have.second_gain = all_gains[1:2]
        factors = (
            2.0 / (3 * width * width) / math.sqrt(width),
            2.0 / (width * width) / math.sqrt(width),
            2.0 / (width * hidden_width) / math.sqrt(width),
            2.0 / (width * hidden_width) / math.sqrt(hidden_width),
        )
        have.betas = totals[:4] * jnp.array(factors, WIDE)

    packed = ((width, rows), LOW)

    def prepare():
        scalars = jnp.concatenate([my_tensor.reshape(1), order ^ my_fsdp]).astype(jnp.int32)

        def kernel(where, student, teacher, x_low, entry, xt_low, to_place, rows_s, rows_t, sems):
            start = pl.multiple_of(where[0] * rows, rows)
            copies = [
                pltpu.make_async_copy(ref.at[pl.ds(start, rows)], to, sems.at[k])
                for k, (ref, to) in enumerate(((student, rows_s), (teacher, rows_t)))
            ]
            for copy in copies:
                copy.start()
            natural = lax.broadcasted_iota(jnp.int32, (width, width), 0)
            place = lax.broadcasted_iota(jnp.int32, (1, width), 1)
            source = place
            for k in range(fsdp):
                inside = (place >= k * depth) & (place < (k + 1) * depth)
                source = jnp.where(inside, place + (where[1 + k] - k) * depth, source)
            to_place[...] = jnp.where(natural == source, 1.0, 0.0).astype(LOW)
            copies[0].wait()
            x = kernel_nn(rows_s[...], to_place[...])
            x_low[...] = x.astype(LOW)
            entry[...] = soft_clip(x).astype(LOW)
            copies[1].wait()
            xt_low[...] = kernel_nn(rows_t[...], to_place[...]).astype(LOW)

        full = ((rows, width), LOW, whole(rows, width))
        have.x_low, have.entry, have.xt_low, have.leave = run.call(
            "place_rows",
            kernel,
            [
                (scalars, SCALARS),
                (student_in, IN_PLACE),
                (teacher_in, IN_PLACE),
            ],
            [full, full, full, ((width, width), LOW, whole(width, width))],
            scratch=[pltpu.VMEM((rows, width), LOW), pltpu.VMEM((rows, width), LOW), pltpu.SemaphoreType.DMA((2,))],
        )

    def prepare_slots():
        units = rows // 64
        first_unit = my_tensor * units

        def kernel(first, sizes, lengths, qid, kid, live_rows):
            for u in range(units):
                unit = first[0] + u
                slot = unit * 64
                size, length = sizes[unit], lengths[unit]
                begin = slot - lax.rem(slot, size)
                here = slice(u * 64, (u + 1) * 64)
                down = slot - begin + lax.broadcasted_iota(jnp.int32, (64, 128), 0)
                kid[here] = jnp.where(down < length, begin, -1)
                live_rows[here] = jnp.where(down < length, 1.0, 0.0)
                across = slot - begin + lax.broadcasted_iota(jnp.int32, (8, 64), 1)
                row = lax.broadcasted_iota(jnp.int32, (8, 64), 0)
                qid[:, here] = jnp.where(row == 0, begin, jnp.where(across < length, 1, 0))

        have.qid, have.kid, have.live_rows = run.call(
            "slots",
            kernel,
            [
                (first_unit.astype(jnp.int32).reshape(1), SCALARS),
                (bucket_size, SCALARS),
                (seq_length, SCALARS),
            ],
            [
                ((8, rows), jnp.int32, whole(8, rows)),
                ((rows, 128), jnp.int32, whole(rows, 128)),
                ((rows, 128), WIDE, whole(rows, 128)),
            ],
        )

    scale = HEAD_DIM ** (-0.5)

    def project_teacher():
        def work(product, refs, here):
            factor = jnp.where(pl.program_id(0) == 0, scale, 1.0)
            return [(product.astype(LOW) * factor.astype(LOW)).astype(LOW)]

        have.proj_t = times_weight(
            run, "project_teacher", have.xt_low, have.w_tqkv, narrow_tiles, work, [], [LOW]
        )[0]

    def project_student():
        def work(product, refs, here):
            factor = jnp.where(pl.program_id(0) == 0, scale, 1.0)
            return [((refs[0][0] * product).astype(LOW) * factor.astype(LOW)).astype(LOW)]

        have.proj_s = times_weight(
            run, "project_student", have.entry, have.w_qkv, narrow_tiles, work,
            [(have.betas, SCALARS)], [LOW],
        )[0]

    def attend(step):
        onto = [have.attended, have.t_attended, have.probs, have.gap] if step else []
        have.attended, have.t_attended, have.probs, have.gap = run_forward(
            run, step, 2, onto, have.qid, have.kid, have.proj_s, have.proj_t
        )

    square = ((rows, width), WIDE)
    square_low = ((rows, width), LOW)

    def close_teacher():
        def work(product, refs, outs, tile):
            here = rows_at(tile)
            normed, _ = norm_parts(refs[0][here].astype(WIDE) + product)
            outs[0][here] = normed
            outs[1][here] = normed.astype(LOW)

        have.t_first, have.t_first_low = times_turned(
            run, "close_teacher", have.t_attended, have.w_tqkv, [3], work,
            [], [have.xt_low], [square, square_low],
        )

    def close_student():
        def work(product, refs, outs, tile):
            betas, gain, x = refs
            here = rows_at(tile)
            normed, size = norm_parts(x[here].astype(WIDE) + betas[1] * product)
            outs[0][here] = normed
            outs[1][here] = jnp.broadcast_to(size, (TILE, 128))
            outs[2][here] = soft_clip(normed * gain[...]).astype(LOW)

        have.n_first, have.r_first, have.middle = times_turned(
            run, "close_student", have.attended, have.w_qkv, [3], work,
            [(have.betas, SCALARS), (have.first_gain, whole(1, width))],
            [have.x_low],
            [square, ((rows, 128), WIDE), square_low],
        )

    def up_teacher():
        def work(product, refs, here):
            return [(product * gelu_cdf(product)).astype(LOW)]

        have.t_hidden = times_weight(
            run, "up_teacher", have.t_first_low, have.w_up, wide_tiles(0), work, [], [LOW]
        )[0]

    def up_student():
        def work(product, refs, here):
            up = refs[0][2] * product
            cdf = gelu_cdf(up)
            return [(up * cdf).astype(LOW), (cdf + up * gelu_density(up)).astype(LOW)]

        have.hidden, have.slope = times_weight(
            run, "up_student", have.middle, have.w_up, wide_tiles(1), work,
            [(have.betas, SCALARS)], [LOW, LOW],
        )

    def down_both():
        parts = have.w_down
        count = len(parts)
        late = [have.t_first, have.n_first, have.live_rows, have.leave]

        def kernel(t_left, s_left, *refs):
            blocks, refs = refs[:count], refs[count:]
            betas, first_gain, second_gain = refs[:3]
            sources = refs[3:7]
            d_second, grad_z, sums, packed = refs[7:11]
            t_total, s_total, weight, t_first, n_first, live_rows, leave, sems = refs[11:]
            j = pl.program_id(0)
            copies = [
                pltpu.make_async_copy(source, to, sems.at[k])
                for k, (source, to) in enumerate(zip(sources, (t_first, n_first, live_rows, leave)))
            ]

            @pl.when(j == 0)
            def _():
                for copy in copies:
                    copy.start()

            row = 0
            for block in blocks:
                weight[pl.ds(row, block.shape[0])] = block[...]
                row += block.shape[0]

            def add(total, left, first):
                product = kernel_nt(left[...], weight[...])

                @pl.when(j == first)
                def _():
                    total[...] = product

                @pl.when(j > first)
                def _():
                    total[...] = total[...] + product

            pl.when(j < tensor)(lambda: add(t_total, t_left, 0))
            pl.when(j >= tensor)(lambda: add(s_total, s_left, tensor))

            @pl.when(j == 2 * tensor - 1)
            def _():
                for copy in copies:
                    copy.wait()
                for tile in range(rows // TILE):
                    here = rows_at(tile)
                    t_result, _ = norm_parts(t_first[here] + t_total[here])
                    normed, size = norm_parts(n_first[here] * first_gain[...] + betas[3] * s_total[here])
                    result = normed * second_gain[...]
                    d_result = jnp.where(live_rows[here][:, 0:1] > 0, result - t_result, 0.0)
                    add_column_sums(sums, d_result * normed, tile)
                    value = norm_back(d_result * second_gain[...], normed, size)
                    d_second[here] = value
                    grad_z[here] = (betas[3] * value).astype(LOW)
                    put_turned(t_result.astype(LOW), leave, packed, tile)
                    put_turned(result.astype(LOW), leave, packed, rows // TILE + tile)

        tiles = pl.BlockSpec((rows, width), lambda j: (0, jnp.clip(j, 0, tensor - 1)))
        later = pl.BlockSpec((rows, width), lambda j: (0, jnp.clip(j - tensor, 0, tensor - 1)))

        def place(j):
            return (0, jnp.where(j < tensor, 2 * j, 2 * (j - tensor) + 1))

        have.d_second, have.grad_z, have.sums_second, have.leaving = run.call(
            "down_both",
            kernel,
            [(have.t_hidden, tiles), (have.hidden, later)]
            + [(part, pl.BlockSpec((part.shape[0], width), place)) for part in parts]
            + [
                (have.betas, SCALARS),
                (have.first_gain, whole(1, width)),
                (have.second_gain, whole(1, width)),
            ]
            + [(value, IN_PLACE) for value in late],
            [
                (shape, dtype, whole(*shape))
                for shape, dtype in (square, square_low, ((8, width), WIDE), ((width, 2 * rows), LOW))
            ],
            grid=(2 * tensor,),
            scratch=[pltpu.VMEM((rows, width), WIDE), pltpu.VMEM((rows, width), WIDE), pltpu.VMEM((width, width), LOW)]
            + [pltpu.VMEM(value.shape, value.dtype) for value in late]
            + [pltpu.SemaphoreType.DMA((4,))],
            flops=4 * rows * width * hidden_width,
            moved=4 * (rows * hidden_width + width * hidden_width),
        )


    def split_one(a, b):
        return tuple(value.reshape(depth, tensor // 2, -1).transpose(1, 0, 2) for value in (a, b))

    def split_qkv(a, b):
        value = jnp.concatenate([a, b], axis=1).reshape(depth, 3, tensor, part).transpose(2, 0, 1, 3)
        value = value.reshape(tensor, depth, 3 * part)
        return value[: tensor // 2], value[tensor // 2 :]

    def share_down():
        return Task(scatter_weight(run, "g_down", have.grad_z, have.hidden, None, keep("grad_down")))

    def back_down():
        def work(product, refs, here):
            return [(refs[0][2] * (product * refs[1][here].astype(WIDE))).astype(LOW)]

        have.grad_u = times_weight(
            run, "back_down", have.grad_z, have.w_down, wide_tiles(1), work,
            [(have.betas, SCALARS), (have.slope, pl.BlockSpec((rows, width), lambda j: (0, j)))],
            [LOW],
        )[0]

    def share_up():
        return Task(scatter_weight(run, "g_up", have.middle, have.grad_u, None, keep("grad_up")))

    def back_up():
        def work(product, refs, outs, tile):
            betas, gain, d_second, n_first, r_first, w_out = refs
            here = rows_at(tile)
            normed = n_first[here]
            d_h = d_second[here] + product * clip_slope(normed * gain[...])
            add_column_sums(outs[3], d_h * normed, tile)
            d_first = norm_back(d_h * gain[...], normed, r_first[here][:, 0:1])
            outs[0][here] = d_first
            grad_o = (betas[1] * d_first).astype(LOW)
            outs[1][here] = grad_o
            outs[2][here] = kernel_nn(grad_o, w_out[...]).astype(LOW)

        have.d_first, have.grad_o, have.d_attended, have.sums_first = times_turned(
            run, "back_up", have.grad_u, have.w_up, wide_tiles(1), work,
            [(have.betas, SCALARS), (have.first_gain, whole(1, width))],
            [have.d_second, have.n_first, have.r_first, (have.w_qkv, 3 * width)],
            [square, square_low, square_low, ((8, width), WIDE)],
        )

    def share_out():
        beside = (have.sums_first, have.sums_second)
        return Task(
            scatter_weight(run, "g_out", have.grad_o, have.attended, split_one, keep("grad_out"), beside)
        )

    def back_attend():
        have.g_all = run_backward(
            run, have.betas, have.proj_s, have.d_attended, have.probs, have.gap
        )

    def share_qkv():
        return Task(scatter_weight(run, "g_qkv", have.entry, have.g_all, split_qkv, keep("grad_qkv"), triple=True))

    def back_entry():
        def work(product, refs, outs, tile):
            here = rows_at(tile)
            x = refs[1][here].astype(WIDE)
            put_turned((refs[0][here] + product * clip_slope(x)).astype(LOW), refs[2], outs[0], tile)

        have.g_leave = times_turned(
            run, "back_entry", have.g_all, have.w_qkv, narrow_tiles, work,
            [], [have.d_first, have.x_low, have.leave], [packed],
        )[0]

    def bring(name, shard, finish_rows):
        return Task(gather_weight(run, name, shard, finish_rows, keep(name)))

    ta = bring("w_tqkv", shard_tqkv, finish_qkv)
    sa = bring("w_qkv", shard_qkv, finish_qkv)
    c = bring("w_up", shard_up, None)
    d = bring("w_down", shard_down, None)
    go_on(ta)
    run.wait(run.shards[0])
    small = Task(gather_small(gains, magnitudes(), small_store))
    go_on(sa)
    go_on(small)
    run.land(small)
    prepare_slots()
    go_on(c)
    go_on(small)
    run.land(small)
    go_on(ta)
    go_on(small)
    prepare()
    run.land(small)
    go_on(sa)
    go_on(ta)
    run.land(ta, only=0)
    run.fence()
    go_on(ta)
    run.land(sa)
    go_on(c)
    run.land(ta)
    go_on(sa)
    go_on(small)
    go_on(ta)
    run.land(ta, only=1)
    run.land(sa, only=0)
    run.fence()
    go_on(ta)
    go_on(sa)
    run.land(sa)
    run.land(small)
    run.land(c)
    run.fence()
    go_on(small)
    go_on(sa)
    go_on(d)
    run.land(sa, only=1)
    run.land(small)
    run.fence()
    finish(small)
    go_on(sa)
    finish(ta)
    go_on(c)
    go_on(c)
    project_teacher()
    go_on(d)
    finish(sa)
    project_student()
    attend(0)
    run.land(c, d)
    run.fence()
    go_on(c)
    go_on(c)
    attend(1)
    go_on(d)
    go_on(d)
    close_teacher()
    run.land(c)
    close_student()
    finish(c)
    run.land(d, only=0)
    up_teacher()
    run.land(d, only=1)
    run.fence()
    go_on(d)
    go_on(d)
    up_student()
    run.land(d)
    run.fence()
    finish(d)
    down_both()
    leaving = Task(leave_columns(run, "arrive", have.leaving, LOW, 2, keep("teacher_out", "student_out")))
    go_on(leaving)
    down = share_down()
    go_on(down)
    back_down()
    up = share_up()
    go_on(up)
    go_on(down)
    go_on(up)
    back_up()
    go_on(down)
    back_attend()
    go_on(down)
    go_on(up)
    qkv = share_qkv()
    go_on(qkv)
    run.land(down, leaving)
    go_on(up)
    go_on(down)
    back_entry()
    g_leave = Task(leave_columns(run, "arrive_grad", have.g_leave, WIDE, 1, keep("input_grad")))
    go_on(g_leave)
    out = share_out()
    go_on(out)
    run.land(down, up)
    go_on(qkv)
    go_on(up)
    go_on(out)
    go_on(qkv)
    finish(leaving)
    go_on(qkv)
    go_on(out)
    finish(g_leave)
    go_on(out)
    finish(qkv)
    finish(out)
    finish(up)
    finish(down)

    def inside(grad, latent):
        return jnp.where(jnp.abs(latent) <= 1.0, grad, 0.0)

    return (
        have.student_out,
        have.teacher_out,
        have.input_grad,
        inside(have.grad_qkv.reshape(depth, 3, part).transpose(1, 0, 2), qkv_latent),
        inside(have.grad_out[:, :part].T, out_latent),
        inside(have.grad_up, up_latent),
        inside(have.grad_down.T, down_latent),
        have.grad_out[:, part],
        have.grad_out[:, part + 1],
    )


def solution(mesh):
    placed = (
        P(FSDP, None),
        P(FSDP, None),
        P(FSDP),
        P(FSDP),
        P(None, FSDP, TENSOR),
        P(TENSOR, FSDP),
        P(FSDP, TENSOR),
        P(TENSOR, FSDP),
        P(FSDP),
        P(FSDP),
        P(None, FSDP, TENSOR),
        P(TENSOR, FSDP),
        P(FSDP, TENSOR),
        P(TENSOR, FSDP),
    )
    return jax.shard_map(
        body,
        mesh=mesh,
        in_specs=placed,
        out_specs=(
            P(FSDP, TENSOR),
            P(FSDP, TENSOR),
            P(FSDP, TENSOR),
            P(None, FSDP, TENSOR),
            P(TENSOR, FSDP),
            P(FSDP, TENSOR),
            P(TENSOR, FSDP),
            P(FSDP),
            P(FSDP),
        ),
        check_vma=False,
    )
```

```python
import functools
import math
import types

import jax
import jax.numpy as jnp
from jax import lax
from jax.experimental import pallas as pl
from jax.experimental.pallas import tpu as pltpu
from jax.sharding import PartitionSpec as P

HEAD_DIM = 64
PAIR = 2 * HEAD_DIM
TILE = 256
CLIP_RANGE = 2.5
ATT_WEIGHT = 0.015625
EPSILON = 1e-06
NEG_FILL = -1000000000.0
LOW = jnp.bfloat16
WIDE = jnp.float32
FSDP = "fsdp"
TENSOR = "tensor"
VMEM_BYTES = 60 * 1024 * 1024
WEIGH = 5


IN_PLACE = pl.BlockSpec(memory_space=pl.ANY)
SCALARS = pl.BlockSpec(memory_space=pltpu.SMEM)


class Task:
    def __init__(self, stages):
        self.stages = stages
        self.arrays = None

    def go_on(self):
        try:
            got = next(self.stages) if self.arrays is None else self.stages.send(self.arrays)
            self.arrays = list(got)
        except StopIteration:
            self.arrays = ()

    def finish(self):
        while self.arrays != ():
            self.go_on()


class Order:
    def __init__(self):
        self.after = []
        self.landing = []
        self.shards = []

    def land(self, *tasks, only=None):
        for task in tasks:
            for k in range(len(task.arrays)):
                if only is None or only == k:
                    self.landing.append((task, k))

    def wait(self, *arrays):
        self.after = self.after + list(arrays)

    def fence(self):
        def kernel(out):
            out[...] = jnp.zeros((8, 128), WIDE)

        self.call("fence", kernel, [], [((8, 128), WIDE, whole(8, 128))])

    def call(self, name, kernel, ins, outs, grid=(1,), scratch=(), flops=0, moved=0, onto=()):
        waits = [value for value in self.after if not any(value is array for array in onto)]
        passed = [task.arrays[k] for task, k in self.landing]
        count, given = len(ins), len(outs)
        skip = len(onto) + len(passed) + len(waits)

        def wrapped(*refs):
            kernel(*refs[:count], *refs[count + skip : count + skip + given], *refs[count + skip + given + len(passed) :])

        aliases = {count + k: k for k in range(len(onto))}
        aliases.update({count + len(onto) + k: given + k for k in range(len(passed))})
        results = pl.pallas_call(
            wrapped,
            grid=grid,
            in_specs=[spec for _, spec in ins] + [IN_PLACE] * skip,
            out_specs=[spec for _, _, spec in outs] + [IN_PLACE] * len(passed),
            out_shape=[jax.ShapeDtypeStruct(shape, dtype) for shape, dtype, _ in outs]
            + [jax.ShapeDtypeStruct(array.shape, array.dtype) for array in passed],
            scratch_shapes=list(scratch),
            input_output_aliases=aliases,
            compiler_params=pltpu.CompilerParams(vmem_limit_bytes=VMEM_BYTES),
            cost_estimate=pl.CostEstimate(flops=flops * WEIGH, bytes_accessed=moved * WEIGH, transcendentals=0),
            name=name,
        )(*[array for array, _ in ins], *onto, *passed, *waits)
        rest = list(results[given:])
        for task, k in self.landing:
            task.arrays[k] = rest.pop(0)
        self.landing = []
        self.after = [results[0]]
        return list(results[:given])


def whole(*shape):
    return pl.BlockSpec(shape, lambda *_: (0,) * len(shape))


def swap(value, axis, bit):
    size = lax.axis_size(axis)
    return lax.ppermute(value, axis, [(i, i ^ bit) for i in range(size)])


def swap_first(value):
    return lax.ppermute(value, FSDP, [(i, i ^ (4 if i % 2 else 2)) for i in range(8)])


def swap_second(value):
    return lax.ppermute(value, FSDP, [(i, i ^ (2 if i % 2 else 4)) for i in range(8)])


def bits_of(axis):
    size = lax.axis_size(axis)
    bits = [1 << k for k in range(size.bit_length() - 1)]
    return [bits[0]] + bits[:0:-1] if bits else []


def order_of(axis):
    order = [0]
    for bit in reversed(bits_of(axis)):
        order = order + [o ^ bit for o in order]
    return order


def two_links(rows):
    return lax.axis_size(FSDP) == 8 and rows % 32 == 0


CHIP_ORDERS = ([0, 2, 4, 6, 1, 5, 3, 7], [0, 4, 2, 6, 1, 3, 5, 7])


def feature_order(depth):
    if not two_links(depth):
        return jnp.array(order_of(FSDP), jnp.int32)
    odd = lax.axis_index(FSDP) & 1
    return jnp.where(odd > 0, jnp.array(CHIP_ORDERS[1], jnp.int32), jnp.array(CHIP_ORDERS[0], jnp.int32))


def reorder(blocks, back):
    plain = order_of(FSDP)
    results = []
    for chip in CHIP_ORDERS:
        if back:
            results.append([blocks[chip.index(m)] for m in plain])
        else:
            results.append([blocks[plain.index(m)] for m in chip])
    odd = lax.axis_index(FSDP) & 1
    return [jnp.where(odd > 0, two, one) for one, two in zip(*results)]


def join_columns(run, name, arrays, moves, columns):
    rows = arrays[0].shape[0]

    def kernel(*refs):
        for k, source, target, count in moves:
            refs[-1][:, target : target + count] = refs[k][:, source : source + count]

    return run.call(
        name,
        kernel,
        [(array, whole(*array.shape)) for array in arrays],
        [((rows, columns), LOW, whole(rows, columns))],
        moved=4 * rows * columns,
    )[0]


def side_by_side(run, name, left, right):
    n = left.shape[1]
    return join_columns(run, name, [left, right], [(0, 0, 0, n), (1, 0, n, n)], 2 * n)


def rows_in_order(run, name, near, far):
    rows, wide = near.shape
    n = wide // 2
    places = lax.axis_index(TENSOR) ^ jnp.array([0, 2, 1, 3], jnp.int32)

    def kernel(where, near_ref, far_ref, out):
        for k in range(4):
            ref = near_ref if k < 2 else far_ref
            start = pl.multiple_of(where[k] * n, 128)
            out[:, pl.ds(start, n)] = ref[:, (k % 2) * n : (k % 2 + 1) * n]

    return run.call(
        name,
        kernel,
        [(places, SCALARS), (near, whole(rows, wide)), (far, whole(rows, wide))],
        [((rows, 2 * wide), LOW, whole(rows, 2 * wide))],
    )[0]


def gather_weight(run, name, shard, finish, store):
    value = shard()
    run.shards.append(value)
    if finish is None:
        (got,) = yield [swap(value, TENSOR, 2)]
        value = side_by_side(run, name + "_join", value, got)
        (got,) = yield [swap(value, TENSOR, 1)]
        mine = rows_in_order(run, name + "_rows", value, got)
    else:
        (got,) = yield [swap(value, TENSOR, 2)]
        value = side_by_side(run, name + "_join", value, got)
        (got,) = yield [swap(value, TENSOR, 1)]
        mine = finish(name + "_rows", value, got)
    if two_links(mine.shape[0]):
        sibling, first = yield [swap(mine, FSDP, 1), swap_first(mine)]
        first, first_other = yield [first, swap_first(sibling)]
        second_other, second = yield [swap(first, FSDP, 1), swap(first_other, FSDP, 1)]
        (both,) = yield [swap_first(second)]
        both_other = swap(both, FSDP, 1)
        store((mine, first, second, both, sibling, second_other, first_other, both_other))
    else:
        for bit in reversed(bits_of(FSDP)):
            mine = jnp.concatenate([mine, swap(mine, FSDP, bit)], axis=0)
        store((mine,))


def add_low(left, right):
    return (left.astype(WIDE) + right.astype(WIDE)).astype(LOW)


def scatter_weight(run, name, left, right, split, store, beside=None, kinds=0):
    rows, width = left.shape
    fsdp = lax.axis_size(FSDP)
    depth = width // fsdp
    columns = right.shape[1]
    middle, half = width // 2, columns // 2
    step = half
    steps = half // step
    side = pl.BlockSpec((rows, step), lambda j: (0, j))
    cost = dict(flops=2 * rows * middle * columns, moved=2 * (rows * columns + 2 * middle * columns))
    added = []
    out_step = step
    if beside is not None:
        added = [(value, whole(8, width)) for value in beside]
        lanes = step // 2
        out_step = 2 * (lanes + 64)
        half = steps * out_step
        columns = 2 * half

    def product(left_ref, right_ref, sums, start):
        value = kernel_tn(left_ref[...], right_ref[...])
        if not sums:
            return value
        turned = [
            jnp.broadcast_to(jnp.sum(ref[:, start : start + middle], axis=0, keepdims=True), (128, middle)).T for ref in sums
        ]
        lane = lax.broadcasted_iota(jnp.int32, (middle, 128), 1)
        more = jnp.where(lane == 0, turned[0], jnp.where(lane == 1, turned[1], 0.0))[:, :64]
        return jnp.concatenate([value[:, :lanes], more, value[:, lanes:], more], axis=1)

    def far_kernel(left_ref, right_ref, *refs):
        refs[-1][...] = product(left_ref, right_ref, refs[:-1], middle).astype(LOW)

    far = run.call(
        name + "_far",
        far_kernel,
        [(left, pl.BlockSpec((rows, middle), lambda j: (0, 1))), (right, side)] + added,
        [((middle, columns), LOW, pl.BlockSpec((middle, out_step), lambda j: (0, j)))],
        grid=(2 * steps,),
        **cost,
    )[0]
    (got,) = yield [swap(far, FSDP, 1)]
    near_ins = [
        (left, pl.BlockSpec((rows, middle), lambda j: (0, 0))),
        (right, side),
        (got, pl.BlockSpec((middle, out_step), lambda j: (0, j))),
    ] + added
    if two_links(depth):
        one = ((depth, columns), LOW, whole(depth, columns))
        at = [slice(k * depth, (k + 1) * depth) for k in range(4)]

        def near_kernel(left_ref, right_ref, got_ref, *refs):
            keep, send = refs[-2:]
            total = (product(left_ref, right_ref, refs[:-2], 0) + got_ref[...].astype(WIDE)).astype(LOW)
            keep[at[0]], keep[at[1]] = total[at[0]], total[at[2]]
            send[at[0]], send[at[1]] = total[at[1]], total[at[3]]

        def second(keep, got, own, onward):
            own[...] = add_low(keep[at[0]], got[at[0]])
            onward[...] = add_low(keep[at[1]], got[at[1]])

        def third(own, got, *outs):
            n = columns // len(outs)
            for k, out in enumerate(outs):
                lanes = slice(k * n, (k + 1) * n)
                out[...] = add_low(own[:, lanes], got[:, lanes])

        def third_split(own, got, keep, send):
            n = columns // (4 * kinds)
            for p in range(4):
                out = keep if p < 2 else send
                for k in range(kinds):
                    lanes = slice((4 * k + p) * n, (4 * k + p + 1) * n)
                    out[at[p % 2], k * n : (k + 1) * n] = add_low(own[:, lanes], got[:, lanes])

        def third_rows(where, own, got, keep, send):
            n = columns // 4
            for k in range(4):
                lanes = slice(k * n, (k + 1) * n)
                row = pl.multiple_of((where[k] & 1) * depth, depth)

                @pl.when(where[k] < 2)
                def _():
                    keep[pl.ds(row, depth)] = add_low(own[:, lanes], got[:, lanes])

                @pl.when(where[k] >= 2)
                def _():
                    send[pl.ds(row, depth)] = add_low(own[:, lanes], got[:, lanes])

        pair = ((2 * depth, columns), LOW, pl.BlockSpec((2 * depth, out_step), lambda j: (0, j)))
        keep, send = run.call(name + "_near", near_kernel, near_ins, [pair] * 2, grid=(2 * steps,), **cost)
        (got,) = yield [swap_first(send)]
        full = whole(2 * depth, columns)
        own, onward = run.call(name + "_add2", second, [(keep, full), (got, full)], [one] * 2, moved=6 * depth * columns)
        (got,) = yield [swap_second(onward)]
        ins = [(own, one[2]), (got, one[2])]
        if split is None:
            shape = (2 * depth, columns // 4)
            m = jnp.arange(4, dtype=jnp.int32) ^ lax.axis_index(TENSOR)
            ins = [((m & 1) * 2 + (m >> 1), SCALARS)] + ins
            here = run.call(
                name + "_add3", third_rows, ins, [(shape, LOW, whole(*shape))] * 2, moved=6 * depth * columns
            )
            split = lambda *parts: tuple(value.reshape(2, depth, -1) for value in parts)
        else:
            shape = (2 * depth, columns // 4) if kinds else (depth, half)
            work = third_split if kinds else third
            here = run.call(name + "_add3", work, ins, [(shape, LOW, whole(*shape))] * 2, moved=6 * depth * columns)
            if kinds:
                split = lambda *parts: tuple(value.reshape(2, depth, -1) for value in parts)
    else:

        def near_kernel(left_ref, right_ref, got_ref, *refs):
            value = product(left_ref, right_ref, refs[:-1], 0)
            refs[-1][...] = (value + got_ref[...].astype(WIDE)).astype(LOW)

        here = run.call(
            name + "_near",
            near_kernel,
            near_ins,
            [((middle, columns), LOW, pl.BlockSpec((middle, out_step), lambda j: (0, j)))],
            grid=(2 * steps,),
            **cost,
        )[0].reshape(fsdp // 2, depth, columns)
        count = fsdp // 2
        for bit in bits_of(FSDP)[1:]:
            count //= 2
            (got,) = yield [swap(here[count:], FSDP, bit)]
            here = add_low(here[:count], got)
        if split is None:
            here = here[0].reshape(depth, 4, -1).transpose(1, 0, 2).reshape(4 * depth, -1)
        else:
            here = (here[0, :, :half], here[0, :, half:])
    if split is None:
        (here,) = yield [lax.psum_scatter(here, TENSOR, scatter_dimension=0, tiled=True)]
        store(here.astype(WIDE))
        return
    keep, send = split(*here)
    for bit in bits_of(TENSOR):
        (got,) = yield [swap(send, TENSOR, bit)]
        total = add_low(keep, got)
        keep, send = total[: total.shape[0] // 2], total[total.shape[0] // 2 :]
    store(total[0].astype(WIDE))


def gather_small(gains, sums, store):
    depth = gains.shape[1]
    block = jnp.concatenate([sums, jnp.pad(gains, ((0, 6), (0, 128 - depth)))], axis=0)[None]
    for bit in reversed(bits_of(FSDP)):
        (got,) = yield [swap(block, FSDP, bit)]
        block = jnp.concatenate([block, got], axis=0)
    parts = [block[k, 8:10, :depth] for k in range(block.shape[0])]
    gains = jnp.concatenate(reorder(parts, False) if two_links(depth) else parts, axis=1)
    sums = block[:, :8]
    while sums.shape[0] > 1:
        sums = sums[: sums.shape[0] // 2] + sums[sums.shape[0] // 2 :]
    sums = sums[0]
    for bit in bits_of(TENSOR):
        (got,) = yield [swap(sums, TENSOR, bit)]
        sums = sums + got
    store(gains, sums[0])


def leave_columns(run, name, value, dtype, count, store):
    size = lax.axis_size(TENSOR)
    (got,) = yield [lax.all_to_all(value, TENSOR, 0, 0, tiled=True)]
    columns, rows = got.shape[0] // size, got.shape[1] // count

    def kernel(ref, *outs):
        for k, out in enumerate(outs):
            out[...] = ref[:, k * rows : (k + 1) * rows].astype(dtype)

    results = run.call(
        name,
        kernel,
        [(got, pl.BlockSpec((columns, count * rows), lambda i: (i, 0)))],
        [((columns, size * rows), dtype, pl.BlockSpec((columns, rows), lambda i: (0, i)))] * count,
        grid=(size,),
        moved=8 * columns * rows,
    )
    store(*[result.T for result in results])


def put_turned(value, natural, out, tile):
    out[:, tile * TILE : (tile + 1) * TILE] = kernel_nt(natural[...], value).astype(LOW)


def dot(left, right):
    return jnp.dot(left, right, preferred_element_type=WIDE)


def dot_tn(left, right):
    return lax.dot_general(left, right, (((0,), (0,)), ((), ())), preferred_element_type=WIDE)


def dot_nt(left, right):
    return lax.dot_general(left, right, (((1,), (1,)), ((), ())), preferred_element_type=WIDE)


def soft_clip(value):
    return CLIP_RANGE * jnp.tanh(value / CLIP_RANGE)


def clip_slope(value):
    bent = jnp.tanh(value / CLIP_RANGE)
    return 1.0 - bent * bent


def norm_parts(value):
    centre = value - jnp.mean(value, axis=-1, keepdims=True)
    scale = lax.rsqrt(jnp.mean(centre * centre, axis=-1, keepdims=True) + EPSILON)
    return centre * scale, scale


def norm_back(grad, normed, scale):
    return scale * (
        grad
        - jnp.mean(grad, axis=-1, keepdims=True)
        - normed * jnp.mean(grad * normed, axis=-1, keepdims=True)
    )


def gelu_cdf(value):
    return 0.5 + 0.5 * lax.erf(value * math.sqrt(0.5))


def gelu_density(value):
    return jnp.exp(-0.5 * value * value) * (1.0 / math.sqrt(2.0 * math.pi))


def kernel_nt(left, right):
    return lax.dot_general(left, right, (((1,), (1,)), ((), ())), preferred_element_type=WIDE)


def kernel_tn(left, right):
    return lax.dot_general(left, right, (((0,), (0,)), ((), ())), preferred_element_type=WIDE)


def kernel_nn(left, right):
    return jnp.dot(left, right, preferred_element_type=WIDE)


def times_weight(run, name, left, parts, tiles, work, extras, outs):
    rows, width = left.shape
    base, stride = tiles[0], tiles[1] - tiles[0]
    count = len(parts)

    def kernel(*refs):
        weight = refs[-1]
        row = 0
        for block in refs[1 : 1 + count]:
            weight[pl.ds(row, block.shape[0])] = block[...]
            row += block.shape[0]
        for r in range(0, rows, TILE):
            here = pl.ds(r, TILE)
            values = work(kernel_nn(refs[0][here], weight[...]), refs[1 + count : 1 + count + len(extras)], here)
            for ref, value in zip(refs[1 + count + len(extras) : -1], values):
                ref[here] = value

    columns = width * len(tiles)
    return run.call(
        name,
        kernel,
        [(left, whole(rows, width))]
        + [(part, pl.BlockSpec((part.shape[0], width), lambda j: (0, base + stride * j))) for part in parts]
        + extras,
        [((rows, columns), dtype, pl.BlockSpec((rows, width), lambda j: (0, j))) for dtype in outs],
        grid=(len(tiles),),
        scratch=[pltpu.VMEM((width, width), LOW)],
        flops=2 * rows * width * columns,
        moved=2 * (rows * width + width * columns + len(outs) * rows * columns),
    )


def times_turned(run, name, left, parts, tiles, work, extras, late, outs):
    rows, wide = left.shape
    width = sum(part.shape[0] for part in parts)
    step = wide // len(tiles)
    base, stride = tiles[0], tiles[1] - tiles[0] if len(tiles) > 1 else 1
    count, more = len(parts), len(extras)
    sources, held = [], []
    for item in late:
        pieces, column = item if isinstance(item, tuple) else ([item], 0)
        columns = pieces[0].shape[1] if column == 0 and not isinstance(item, tuple) else width
        row = 0
        for piece in pieces:
            sources.append((piece, len(held), row, column, columns))
            row += piece.shape[0]
        held.append(pltpu.VMEM((row, columns), pieces[0].dtype))
    first_late = 1 + count + more
    first_out = first_late + len(sources)
    first_held = first_out + len(outs) + 2

    def kernel(*refs):
        total, weight = refs[first_out + len(outs)], refs[first_out + len(outs) + 1]
        scratch, sems = refs[first_held:-1], refs[-1]
        j = pl.program_id(0)
        copies = []
        for k, (piece, to, row, column, columns) in enumerate(sources):
            copies.append(
                pltpu.make_async_copy(
                    refs[first_late + k].at[:, pl.ds(column, columns)],
                    scratch[to].at[pl.ds(row, piece.shape[0])],
                    sems.at[k],
                )
            )

        @pl.when(j == 0)
        def _():
            for copy in copies:
                copy.start()

        row = 0
        for block in refs[1 : 1 + count]:
            weight[pl.ds(row, block.shape[0])] = block[...]
            row += block.shape[0]
        product = kernel_nt(refs[0][...], weight[...])

        @pl.when(j == 0)
        def _():
            total[...] = product

        @pl.when(j > 0)
        def _():
            total[...] = total[...] + product

        @pl.when(j == len(tiles) - 1)
        def _():
            for copy in copies:
                copy.wait()
            for tile in range(rows // TILE):
                work(
                    total[pl.ds(tile * TILE, TILE)],
                    list(refs[1 + count : first_late]) + list(scratch),
                    refs[first_out : first_out + len(outs)],
                    tile,
                )

    return run.call(
        name,
        kernel,
        [(left, pl.BlockSpec((rows, step), lambda j: (0, j)))]
        + [(part, pl.BlockSpec((part.shape[0], step), lambda j: (0, base + stride * j))) for part in parts]
        + extras
        + [(piece, IN_PLACE) for piece, _, _, _, _ in sources],
        [(shape, dtype, whole(*shape)) for shape, dtype in outs],
        grid=(len(tiles),),
        scratch=[pltpu.VMEM((rows, width), WIDE), pltpu.VMEM((width, step), LOW)]
        + held
        + [pltpu.SemaphoreType.DMA((max(len(sources), 1),))],
        flops=2 * rows * width * wide,
        moved=2 * (rows * wide + width * wide),
    )


def rows_at(tile):
    return pl.ds(tile * TILE, TILE)


def tile_rows(columns):
    return pl.BlockSpec((TILE, columns), lambda i: (i, 0))


def add_column_sums(ref, value, tile):
    total = jnp.sum(value.reshape(value.shape[0] // 8, 8, value.shape[1]), axis=0)
    ref[...] = total if tile == 0 else ref[...] + total


def both_heads(value):
    first = lax.broadcasted_iota(jnp.int32, (1, PAIR), 1) < HEAD_DIM
    zero = jnp.zeros((), value.dtype)
    return jnp.concatenate([jnp.where(first, value, zero), jnp.where(first, zero, value)], axis=0)


def own_heads(value):
    return jnp.concatenate([value[:HEAD_DIM, :TILE], value[HEAD_DIM:, TILE:]], axis=0).T


def attend_forward(qid, kid, qs, ks, vs, qt, kt, vt, os, ot, probs_out, gap_out):
    keep = kid[:, 0:1] == qid[0:1, :]
    both = keep & (qid[1:2, :] > 0)
    bias = jnp.where(keep, 0.0, NEG_FILL)
    bias = jnp.concatenate([bias, bias], axis=1)
    seen = jnp.where(both, 1.0, 0.0)
    seen = jnp.concatenate([seen, seen], axis=1)

    def soft(score):
        masked = score + bias
        expo = jnp.exp(masked - jnp.max(masked, axis=0, keepdims=True))
        return (expo * (1.0 / jnp.sum(expo, axis=0, keepdims=True))).astype(LOW)

    for p in range(qs.shape[1] // PAIR):
        here = slice(p * PAIR, (p + 1) * PAIR)
        score_s = kernel_nt(ks[:, here], both_heads(qs[:, here]))
        score_t = kernel_nt(kt[:, here], both_heads(qt[:, here]))
        gap_out[0, p] = ((score_s - score_t) * seen).astype(LOW)
        probs = soft(score_s)
        probs_out[0, p] = probs
        os[:, here] = own_heads(kernel_tn(vs[:, here], probs)).astype(LOW)
        ot[:, here] = own_heads(kernel_tn(vt[:, here], soft(score_t))).astype(LOW)


def attend_backward(betas, proj, grad, probs, gap, out):
    width = grad.shape[1]
    up = jnp.asarray(1.0 / ATT_WEIGHT, LOW)
    b = betas[0] * ATT_WEIGHT
    scale = HEAD_DIM ** (-0.5)
    for p in range(width // PAIR):
        at_q = slice(p * PAIR, (p + 1) * PAIR)
        at_k = slice(width + p * PAIR, width + (p + 1) * PAIR)
        at_v = slice(2 * width + p * PAIR, 2 * width + (p + 1) * PAIR)
        grad_two = both_heads(grad[:, at_q] * up)
        prob_low = probs[0, p]
        prob = prob_low.astype(WIDE)
        weighted = prob * kernel_nt(proj[:, at_v], grad_two)
        inner = jnp.sum(weighted, axis=0, keepdims=True)
        d_score = (weighted - prob * inner + gap[0, p].astype(WIDE)).astype(LOW)
        out[:, at_v] = (b * kernel_nn(prob_low, grad_two)).astype(LOW)
        out[:, at_k] = (b * kernel_nn(d_score, both_heads(proj[:, at_q]))).astype(LOW)
        out[:, at_q] = own_heads((b * scale) * kernel_tn(proj[:, at_k], d_score)).astype(LOW)


def run_forward(run, step, steps, onto, qid, kid, proj_s, proj_t):
    rows, wide = proj_s.shape
    width = wide // 3
    pairs = width // PAIR
    tiles = rows // TILE

    def part(j):
        return pl.BlockSpec((TILE, width // steps), lambda b: (b, j * steps + step))

    square = pl.BlockSpec((1, pairs // steps, TILE, 2 * TILE), lambda b: (b, step, 0, 0))
    return run.call(
        "attend_forward",
        attend_forward,
        [(qid, pl.BlockSpec((8, TILE), lambda b: (0, b))), (kid, pl.BlockSpec((TILE, 128), lambda b: (b, 0)))]
        + [(value, part(j)) for value in (proj_s, proj_t) for j in range(3)],
        [((rows, width), LOW, part(0))] * 2 + [((tiles, pairs, TILE, 2 * TILE), LOW, square)] * 2,
        grid=(tiles,),
        flops=32 * rows * TILE * width // steps,
        moved=8 * rows * wide // steps,
        onto=onto,
    )


def run_backward(run, betas, proj_s, grad, probs, gap):
    rows, wide = proj_s.shape
    width = wide // 3
    pairs = width // PAIR
    square = pl.BlockSpec((1, pairs, TILE, 2 * TILE), lambda b: (b, 0, 0, 0))
    return run.call(
        "attend_backward",
        attend_backward,
        [(betas, SCALARS), (proj_s, tile_rows(wide)), (grad, tile_rows(width)), (probs, square), (gap, square)],
        [((rows, wide), LOW, tile_rows(wide))],
        grid=(rows // TILE,),
        flops=16 * rows * TILE * width,
        moved=8 * rows * wide,
    )[0]


def body(
    student_in,
    teacher_in,
    bucket_size,
    seq_length,
    qkv_latent,
    out_latent,
    up_latent,
    down_latent,
    gain_attn,
    gain_ffn,
    teach_qkv,
    teach_out,
    teach_up,
    teach_down,
):
    width = student_in.shape[1]
    fsdp = lax.axis_size(FSDP)
    tensor = lax.axis_size(TENSOR)
    rows = student_in.shape[0] // tensor
    depth = width // fsdp
    hidden_width = up_latent.shape[1] * tensor
    my_fsdp = lax.axis_index(FSDP)
    my_tensor = lax.axis_index(TENSOR)
    first_row = my_tensor * rows
    order = feature_order(depth)
    order_t = order_of(TENSOR)

    have = types.SimpleNamespace()
    run = Order()

    def keep(*names):
        def store(*values):
            for name, value in zip(names, values):
                setattr(have, name, value)

        return store

    def go_on(*tasks):
        for task in tasks:
            task.go_on()

    def finish(*tasks):
        for task in tasks:
            task.finish()

    gains = jnp.stack([gain_attn, gain_ffn]).astype(WIDE)

    def magnitudes():
        latents = (qkv_latent.reshape(-1, qkv_latent.shape[2]), out_latent, up_latent, down_latent)

        def kernel(*refs):
            lane = lax.broadcasted_iota(jnp.int32, (8, 128), 1)
            total = jnp.zeros((8, 128), WIDE)
            for k in range(4):
                total = jnp.where(lane == k, jnp.sum(jnp.abs(refs[k][...])), total)
            refs[4][...] = total

        return run.call(
            "magnitudes", kernel, [(value, whole(*value.shape)) for value in latents], [((8, 128), WIDE, whole(8, 128))]
        )[0]

    def pack_qkv(value):
        return value.astype(LOW).transpose(1, 0, 2).reshape(depth, -1)

    part = width // tensor

    def finish_qkv(name, near, far):
        moves = []
        for p in range(tensor):
            for k in range(4):
                moves.append((p // 2, (p % 2) * 4 * part + k * part, k * width + p * part, part))
        return join_columns(run, name, [near, far], moves, 4 * width)

    narrow_tiles = [0, 1, 2]

    def wide_tiles(which):
        return [2 * p + which for p in range(tensor)]

    def signs(value):
        return jnp.sign(value).astype(LOW)


    def shard_tqkv():
        return jnp.concatenate([pack_qkv(teach_qkv), teach_out.T], axis=1)

    def shard_qkv():
        return jnp.concatenate([pack_qkv(signs(qkv_latent)), signs(out_latent).T], axis=1)

    def pack_signs(name, teach, latent):
        def kernel(teach_ref, latent_ref, out):
            value = latent_ref[...]
            n = value.shape[1]
            out[:, :n] = teach_ref[...]
            out[:, n:] = jnp.where(value > 0, 1.0, jnp.where(value < 0, -1.0, 0.0)).astype(LOW)

        r, n = teach.shape
        return run.call(
            name, kernel, [(teach, whole(r, n)), (latent, whole(r, n))], [((r, 2 * n), LOW, whole(r, 2 * n))]
        )[0]

    def shard_up():
        return pack_signs("pack_up", teach_up, up_latent)

    def shard_down():
        return pack_signs("pack_down", teach_down.T, down_latent.T)

    def small_store(all_gains, totals):
        have.first_gain = all_gains[0:1]
        have.second_gain = all_gains[1:2]
        factors = (
            2.0 / (3 * width * width) / math.sqrt(width),
            2.0 / (width * width) / math.sqrt(width),
            2.0 / (width * hidden_width) / math.sqrt(width),
            2.0 / (width * hidden_width) / math.sqrt(hidden_width),
        )
        have.betas = totals[:4] * jnp.array(factors, WIDE)

    packed = ((width, rows), LOW)

    def prepare():
        scalars = jnp.concatenate([my_tensor.reshape(1), order ^ my_fsdp]).astype(jnp.int32)

        def kernel(where, student, teacher, x_low, entry, xt_low, to_place, rows_s, rows_t, sems):
            start = pl.multiple_of(where[0] * rows, rows)
            copies = [
                pltpu.make_async_copy(ref.at[pl.ds(start, rows)], to, sems.at[k])
                for k, (ref, to) in enumerate(((student, rows_s), (teacher, rows_t)))
            ]
            for copy in copies:
                copy.start()
            natural = lax.broadcasted_iota(jnp.int32, (width, width), 0)
            place = lax.broadcasted_iota(jnp.int32, (1, width), 1)
            source = place
            for k in range(fsdp):
                inside = (place >= k * depth) & (place < (k + 1) * depth)
                source = jnp.where(inside, place + (where[1 + k] - k) * depth, source)
            to_place[...] = jnp.where(natural == source, 1.0, 0.0).astype(LOW)
            copies[0].wait()
            x = kernel_nn(rows_s[...], to_place[...])
            x_low[...] = x.astype(LOW)
            entry[...] = soft_clip(x).astype(LOW)
            copies[1].wait()
            xt_low[...] = kernel_nn(rows_t[...], to_place[...]).astype(LOW)

        full = ((rows, width), LOW, whole(rows, width))
        have.x_low, have.entry, have.xt_low, have.leave = run.call(
            "place_rows",
            kernel,
            [
                (scalars, SCALARS),
                (student_in, IN_PLACE),
                (teacher_in, IN_PLACE),
            ],
            [full, full, full, ((width, width), LOW, whole(width, width))],
            scratch=[pltpu.VMEM((rows, width), LOW), pltpu.VMEM((rows, width), LOW), pltpu.SemaphoreType.DMA((2,))],
        )

    def prepare_slots():
        units = rows // 64
        first_unit = my_tensor * units

        def kernel(first, sizes, lengths, qid, kid, live_rows):
            for u in range(units):
                unit = first[0] + u
                slot = unit * 64
                size, length = sizes[unit], lengths[unit]
                begin = slot - lax.rem(slot, size)
                here = slice(u * 64, (u + 1) * 64)
                down = slot - begin + lax.broadcasted_iota(jnp.int32, (64, 128), 0)
                kid[here] = jnp.where(down < length, begin, -1)
                live_rows[here] = jnp.where(down < length, 1.0, 0.0)
                across = slot - begin + lax.broadcasted_iota(jnp.int32, (8, 64), 1)
                row = lax.broadcasted_iota(jnp.int32, (8, 64), 0)
                qid[:, here] = jnp.where(row == 0, begin, jnp.where(across < length, 1, 0))

        have.qid, have.kid, have.live_rows = run.call(
            "slots",
            kernel,
            [
                (first_unit.astype(jnp.int32).reshape(1), SCALARS),
                (bucket_size, SCALARS),
                (seq_length, SCALARS),
            ],
            [
                ((8, rows), jnp.int32, whole(8, rows)),
                ((rows, 128), jnp.int32, whole(rows, 128)),
                ((rows, 128), WIDE, whole(rows, 128)),
            ],
        )

    scale = HEAD_DIM ** (-0.5)

    def project_teacher():
        def work(product, refs, here):
            factor = jnp.where(pl.program_id(0) == 0, scale, 1.0)
            return [(product.astype(LOW) * factor.astype(LOW)).astype(LOW)]

        have.proj_t = times_weight(
            run, "project_teacher", have.xt_low, have.w_tqkv, narrow_tiles, work, [], [LOW]
        )[0]

    def project_student():
        def work(product, refs, here):
            factor = jnp.where(pl.program_id(0) == 0, scale, 1.0)
            return [((refs[0][0] * product).astype(LOW) * factor.astype(LOW)).astype(LOW)]

        have.proj_s = times_weight(
            run, "project_student", have.entry, have.w_qkv, narrow_tiles, work,
            [(have.betas, SCALARS)], [LOW],
        )[0]

    def attend(step):
        onto = [have.attended, have.t_attended, have.probs, have.gap] if step else []
        have.attended, have.t_attended, have.probs, have.gap = run_forward(
            run, step, 2, onto, have.qid, have.kid, have.proj_s, have.proj_t
        )

    square = ((rows, width), WIDE)
    square_low = ((rows, width), LOW)

    def close_teacher():
        def work(product, refs, outs, tile):
            here = rows_at(tile)
            normed, _ = norm_parts(refs[0][here].astype(WIDE) + product)
            outs[0][here] = normed
            outs[1][here] = normed.astype(LOW)

        have.t_first, have.t_first_low = times_turned(
            run, "close_teacher", have.t_attended, have.w_tqkv, [3], work,
            [], [have.xt_low], [square, square_low],
        )

    def close_student():
        def work(product, refs, outs, tile):
            betas, gain, x = refs
            here = rows_at(tile)
            normed, size = norm_parts(x[here].astype(WIDE) + betas[1] * product)
            outs[0][here] = normed
            outs[1][here] = jnp.broadcast_to(size, (TILE, 128))
            outs[2][here] = soft_clip(normed * gain[...]).astype(LOW)

        have.n_first, have.r_first, have.middle = times_turned(
            run, "close_student", have.attended, have.w_qkv, [3], work,
            [(have.betas, SCALARS), (have.first_gain, whole(1, width))],
            [have.x_low],
            [square, ((rows, 128), WIDE), square_low],
        )

    def up_teacher():
        def work(product, refs, here):
            return [(product * gelu_cdf(product)).astype(LOW)]

        have.t_hidden = times_weight(
            run, "up_teacher", have.t_first_low, have.w_up, wide_tiles(0), work, [], [LOW]
        )[0]

    def up_student():
        def work(product, refs, here):
            up = refs[0][2] * product
            cdf = gelu_cdf(up)
            return [(up * cdf).astype(LOW), (cdf + up * gelu_density(up)).astype(LOW)]

        have.hidden, have.slope = times_weight(
            run, "up_student", have.middle, have.w_up, wide_tiles(1), work,
            [(have.betas, SCALARS)], [LOW, LOW],
        )

    def down_both():
        parts = have.w_down
        count = len(parts)
        late = [have.t_first, have.n_first, have.live_rows, have.leave]

        def kernel(t_left, s_left, *refs):
            blocks, refs = refs[:count], refs[count:]
            betas, first_gain, second_gain = refs[:3]
            sources = refs[3:7]
            d_second, grad_z, sums, packed = refs[7:11]
            t_total, s_total, weight, t_first, n_first, live_rows, leave, sems = refs[11:]
            j = pl.program_id(0)
            copies = [
                pltpu.make_async_copy(source, to, sems.at[k])
                for k, (source, to) in enumerate(zip(sources, (t_first, n_first, live_rows, leave)))
            ]

            @pl.when(j == 0)
            def _():
                for copy in copies:
                    copy.start()

            row = 0
            for block in blocks:
                weight[pl.ds(row, block.shape[0])] = block[...]
                row += block.shape[0]

            def add(total, left, first):
                product = kernel_nt(left[...], weight[...])

                @pl.when(j == first)
                def _():
                    total[...] = product

                @pl.when(j > first)
                def _():
                    total[...] = total[...] + product

            pl.when(j < tensor)(lambda: add(t_total, t_left, 0))
            pl.when(j >= tensor)(lambda: add(s_total, s_left, tensor))

            @pl.when(j == 2 * tensor - 1)
            def _():
                for copy in copies:
                    copy.wait()
                for tile in range(rows // TILE):
                    here = rows_at(tile)
                    t_result, _ = norm_parts(t_first[here] + t_total[here])
                    normed, size = norm_parts(n_first[here] * first_gain[...] + betas[3] * s_total[here])
                    result = normed * second_gain[...]
                    d_result = jnp.where(live_rows[here][:, 0:1] > 0, result - t_result, 0.0)
                    add_column_sums(sums, d_result * normed, tile)
                    value = norm_back(d_result * second_gain[...], normed, size)
                    d_second[here] = value
                    grad_z[here] = (betas[3] * value).astype(LOW)
                    put_turned(t_result.astype(LOW), leave, packed, tile)
                    put_turned(result.astype(LOW), leave, packed, rows // TILE + tile)

        tiles = pl.BlockSpec((rows, width), lambda j: (0, jnp.clip(j, 0, tensor - 1)))
        later = pl.BlockSpec((rows, width), lambda j: (0, jnp.clip(j - tensor, 0, tensor - 1)))

        def place(j):
            return (0, jnp.where(j < tensor, 2 * j, 2 * (j - tensor) + 1))

        have.d_second, have.grad_z, have.sums_second, have.leaving = run.call(
            "down_both",
            kernel,
            [(have.t_hidden, tiles), (have.hidden, later)]
            + [(part, pl.BlockSpec((part.shape[0], width), place)) for part in parts]
            + [
                (have.betas, SCALARS),
                (have.first_gain, whole(1, width)),
                (have.second_gain, whole(1, width)),
            ]
            + [(value, IN_PLACE) for value in late],
            [
                (shape, dtype, whole(*shape))
                for shape, dtype in (square, square_low, ((8, width), WIDE), ((width, 2 * rows), LOW))
            ],
            grid=(2 * tensor,),
            scratch=[pltpu.VMEM((rows, width), WIDE), pltpu.VMEM((rows, width), WIDE), pltpu.VMEM((width, width), LOW)]
            + [pltpu.VMEM(value.shape, value.dtype) for value in late]
            + [pltpu.SemaphoreType.DMA((4,))],
            flops=4 * rows * width * hidden_width,
            moved=4 * (rows * hidden_width + width * hidden_width),
        )


    def split_one(a, b):
        return tuple(value.reshape(depth, tensor // 2, -1).transpose(1, 0, 2) for value in (a, b))

    def split_qkv(a, b):
        value = jnp.concatenate([a, b], axis=1).reshape(depth, 3, tensor, part).transpose(2, 0, 1, 3)
        value = value.reshape(tensor, depth, 3 * part)
        return value[: tensor // 2], value[tensor // 2 :]

    def share_down():
        return Task(scatter_weight(run, "g_down", have.grad_z, have.hidden, None, keep("grad_down")))

    def back_down():
        def work(product, refs, here):
            return [(refs[0][2] * (product * refs[1][here].astype(WIDE))).astype(LOW)]

        have.grad_u = times_weight(
            run, "back_down", have.grad_z, have.w_down, wide_tiles(1), work,
            [(have.betas, SCALARS), (have.slope, pl.BlockSpec((rows, width), lambda j: (0, j)))],
            [LOW],
        )[0]

    def share_up():
        return Task(scatter_weight(run, "g_up", have.middle, have.grad_u, None, keep("grad_up")))

    def back_up():
        def work(product, refs, outs, tile):
            betas, gain, d_second, n_first, r_first, w_out = refs
            here = rows_at(tile)
            normed = n_first[here]
            d_h = d_second[here] + product * clip_slope(normed * gain[...])
            add_column_sums(outs[3], d_h * normed, tile)
            d_first = norm_back(d_h * gain[...], normed, r_first[here][:, 0:1])
            outs[0][here] = d_first
            grad_o = (betas[1] * d_first).astype(LOW)
            outs[1][here] = grad_o
            outs[2][here] = kernel_nn(grad_o, w_out[...]).astype(LOW)

        have.d_first, have.grad_o, have.d_attended, have.sums_first = times_turned(
            run, "back_up", have.grad_u, have.w_up, wide_tiles(1), work,
            [(have.betas, SCALARS), (have.first_gain, whole(1, width))],
            [have.d_second, have.n_first, have.r_first, (have.w_qkv, 3 * width)],
            [square, square_low, square_low, ((8, width), WIDE)],
        )

    def share_out():
        beside = (have.sums_first, have.sums_second)
        return Task(
            scatter_weight(run, "g_out", have.grad_o, have.attended, split_one, keep("grad_out"), beside, 1)
        )

    def back_attend():
        have.g_all = run_backward(
            run, have.betas, have.proj_s, have.d_attended, have.probs, have.gap
        )

    def share_qkv():
        return Task(scatter_weight(run, "g_qkv", have.entry, have.g_all, split_qkv, keep("grad_qkv"), kinds=3))

    def back_entry():
        def work(product, refs, outs, tile):
            here = rows_at(tile)
            x = refs[1][here].astype(WIDE)
            put_turned((refs[0][here] + product * clip_slope(x)).astype(LOW), refs[2], outs[0], tile)

        have.g_leave = times_turned(
            run, "back_entry", have.g_all, have.w_qkv, narrow_tiles, work,
            [], [have.d_first, have.x_low, have.leave], [packed],
        )[0]

    def bring(name, shard, finish_rows):
        return Task(gather_weight(run, name, shard, finish_rows, keep(name)))

    ta = bring("w_tqkv", shard_tqkv, finish_qkv)
    sa = bring("w_qkv", shard_qkv, finish_qkv)
    c = bring("w_up", shard_up, None)
    d = bring("w_down", shard_down, None)
    go_on(ta)
    run.wait(run.shards[0])
    small = Task(gather_small(gains, magnitudes(), small_store))
    go_on(sa)
    go_on(small)
    run.land(small)
    prepare_slots()
    go_on(c)
    go_on(small)
    run.land(small)
    go_on(ta)
    go_on(small)
    prepare()
    run.land(small)
    go_on(sa)
    go_on(ta)
    run.land(ta, only=0)
    run.fence()
    go_on(ta)
    run.land(sa)
    go_on(c)
    run.land(ta)
    go_on(sa)
    go_on(small)
    go_on(ta)
    run.land(ta, only=1)
    run.land(sa, only=0)
    run.fence()
    go_on(ta)
    go_on(sa)
    run.land(sa)
    run.land(small)
    run.land(c)
    run.fence()
    go_on(small)
    go_on(sa)
    go_on(d)
    run.land(sa, only=1)
    run.land(small)
    run.fence()
    finish(small)
    go_on(sa)
    finish(ta)
    go_on(c)
    go_on(c)
    project_teacher()
    go_on(d)
    finish(sa)
    project_student()
    attend(0)
    run.land(c, d)
    run.fence()
    go_on(c)
    go_on(c)
    attend(1)
    go_on(d)
    go_on(d)
    close_teacher()
    run.land(c)
    close_student()
    finish(c)
    run.land(d, only=0)
    up_teacher()
    run.land(d, only=1)
    run.fence()
    go_on(d)
    go_on(d)
    up_student()
    run.land(d)
    run.fence()
    finish(d)
    down_both()
    leaving = Task(leave_columns(run, "arrive", have.leaving, LOW, 2, keep("teacher_out", "student_out")))
    go_on(leaving)
    down = share_down()
    go_on(down)
    back_down()
    up = share_up()
    go_on(up)
    go_on(down)
    go_on(up)
    back_up()
    go_on(down)
    back_attend()
    go_on(down)
    go_on(up)
    qkv = share_qkv()
    go_on(qkv)
    run.land(down, leaving)
    go_on(up)
    go_on(down)
    back_entry()
    g_leave = Task(leave_columns(run, "arrive_grad", have.g_leave, WIDE, 1, keep("input_grad")))
    go_on(g_leave)
    out = share_out()
    go_on(out)
    run.land(down, up)
    go_on(qkv)
    go_on(up)
    go_on(out)
    go_on(qkv)
    finish(leaving)
    go_on(qkv)
    go_on(out)
    finish(g_leave)
    go_on(out)
    finish(qkv)
    finish(out)
    finish(up)
    finish(down)

    def inside(grad, latent):
        return jnp.where(jnp.abs(latent) <= 1.0, grad, 0.0)

    return (
        have.student_out,
        have.teacher_out,
        have.input_grad,
        inside(have.grad_qkv.reshape(depth, 3, part).transpose(1, 0, 2), qkv_latent),
        inside(have.grad_out[:, :part].T, out_latent),
        inside(have.grad_up, up_latent),
        inside(have.grad_down.T, down_latent),
        have.grad_out[:, part],
        have.grad_out[:, part + 1],
    )


def solution(mesh):
    placed = (
        P(FSDP, None),
        P(FSDP, None),
        P(FSDP),
        P(FSDP),
        P(None, FSDP, TENSOR),
        P(TENSOR, FSDP),
        P(FSDP, TENSOR),
        P(TENSOR, FSDP),
        P(FSDP),
        P(FSDP),
        P(None, FSDP, TENSOR),
        P(TENSOR, FSDP),
        P(FSDP, TENSOR),
        P(TENSOR, FSDP),
    )
    return jax.shard_map(
        body,
        mesh=mesh,
        in_specs=placed,
        out_specs=(
            P(FSDP, TENSOR),
            P(FSDP, TENSOR),
            P(FSDP, TENSOR),
            P(None, FSDP, TENSOR),
            P(TENSOR, FSDP),
            P(FSDP, TENSOR),
            P(TENSOR, FSDP),
            P(FSDP),
            P(FSDP),
        ),
        check_vma=False,
    )
```
